256 devices in a mesh: scene: 16 (over y, x), tile: 16 (over z, core).
Axes of the slice: x: 4, y: 4, z: 8, core: 2. Of those that a mesh axis runs over, the one named last changes fastest.
Arguments:
- feats: bfloat16 [256, 32, 32, 1024], P('scene', 'tile'), may hold values from -6 to 6
- occupancy: int32 [256, 4, 4, 4], P('scene'), may hold values from 0 to 1, as said below
- assign: int32 [16, 16], P('scene'), may hold values from 0 to 15, each once within a row
- w_first: bfloat16 [864, 64], replicated, may hold values from -0.21875 to 0.21875
- w_second: bfloat16 [1728, 64], replicated, may hold values from -0.15625 to 0.15625
- grad_out: bfloat16 [256, 16, 16, 1024], P(('scene', 'tile')), may hold values from -6 to 6
Outputs:
- decoded: bfloat16 [256, 16, 16, 1024], P(('scene', 'tile'))
- grad_first: float32 [864, 64], replicated
- grad_second: float32 [1728, 64], replicated
The draws below stay inside these ranges and needn't reach their ends.
Inputs may be any that keep to these rules, and one draw needn't show every extreme that they name: Each row of assign names every tile index once. `occupancy`: in each scene, the bricks that share one first brick index hold at most 2 occupied ones, and in every scene some such row holds exactly 2.
All inputs are finite; a program needn't handle non-finite values.
Results may differ from the reference program's by a relative error of at most 0.006.
Values may be sent and summed in bfloat16 or wider, within the bound.
A program may use at most 128 MiB of HBM per device.

```python
import math
import jax
import jax.numpy as jnp
from jax import lax

C_FULL = 32
C_HALF = 64
SX = 32
SY = 32
SZ = 32
BRICK = 8
OCC = 2
SCENES = 256
HX = 16
HY = 16
HZ = 16
N_SCENE = 16
N_TILE = 16


def draw_occupancy(key, part):
    nbx = SX // BRICK
    nrow = SY // BRICK * (SZ // BRICK)
    key_count = jax.random.fold_in(key, 11)
    key_force = jax.random.fold_in(key, 12)
    key_score = jax.random.fold_in(key, 13)
    counts = jax.random.randint(key_count, (SCENES, nbx), 0, OCC + 1).astype(jnp.int32)
    forced = jax.random.randint(key_force, (SCENES,), 0, nbx).astype(jnp.int32)
    columns = jnp.arange(nbx, dtype=jnp.int32)
    counts = jnp.where(columns[None, :] == forced[:, None], OCC, counts).astype(jnp.int32)
    scores = jax.random.randint(key_score, (SCENES, nbx, nrow), 0, 1 << 20).astype(jnp.int32) * nrow + jnp.arange(nrow, dtype=jnp.int32)
    order = jnp.argsort(scores, axis=-1)
    ranks = jnp.argsort(order, axis=-1).astype(jnp.int32)
    occupied = (ranks < counts[:, :, None]).astype(jnp.int32)
    return occupied.reshape(SCENES, nbx, SY // BRICK, SZ // BRICK)


def block_levels(rng, shape, pieces, smallest, largest):
    level = 1.0
    for axis_at, blocks in pieces:
        heights = jax.random.uniform(jax.random.fold_in(jax.random.fold_in(rng, 6), axis_at), (blocks,), jnp.float32, smallest / len(pieces), largest / len(pieces))
        level = level * jnp.repeat(jnp.exp(heights), shape[axis_at] // blocks).reshape((-1,) + (1,) * (len(shape) - 1 - axis_at))
    return level


def noise(key, shape, spread, most, shards=(), kind=jnp.bfloat16):
    gain = block_levels(key, shape, shards, -0.22, 0.18) if shards else 1.0
    result = jax.random.normal(key, shape, jnp.float32) * spread * gain
    return jnp.minimum(jnp.maximum(result, -most), most).astype(kind)


def setup_inputs(seed: int = 0) -> dict:
    splits = jax.random.split(jax.random.key(seed), 7)
    return {
        "feats": noise(splits[0], (SCENES, SX, SY, SZ * C_FULL), 1.0, 6.0, ((0, 16), (1, 16))),
        "occupancy": draw_occupancy(jax.random.fold_in(splits[6], 71), 0),
        "assign": jax.vmap(lambda own: jax.random.permutation(own, N_TILE))(jax.random.split(splits[2], N_SCENE)).reshape((N_SCENE, N_TILE)).astype(jnp.int32),
        "w_first": noise(splits[3], (27 * C_FULL, C_HALF), (27 * C_FULL) ** -0.5, 0.21875),
        "w_second": noise(splits[4], (27 * C_HALF, C_HALF), (27 * C_HALF) ** -0.5, 0.15625),
        "grad_out": noise(splits[5], (SCENES, HX, HY, HZ * C_HALF), 1.0, 6.0, ((0, 256),)),
    }


def upsample(grid, factor):
    grid = jnp.repeat(grid, factor, axis=-3)
    grid = jnp.repeat(grid, factor, axis=-2)
    return jnp.repeat(grid, factor, axis=-1)

def convolve(lhs, rhs, strides, padding, spec):
    return lax.conv_general_dilated(lhs, rhs, strides, padding, dimension_numbers=('NDHWC', spec, 'NDHWC'), preferred_element_type=jnp.float32)

def kernel_grad(lhs, rhs, dilation):
    return lax.conv_general_dilated(lhs, rhs, (1, 1, 1), 'VALID', rhs_dilation=(dilation, dilation, dilation), dimension_numbers=('CDHWN', 'IDHWO', 'DHWNC'), preferred_element_type=jnp.float32)

def silu_slope(value):
    sig_value = jax.nn.sigmoid(value)
    return sig_value * (1.0 + value * (1.0 - sig_value))

def reference(feats, occupancy, assign, w_first, w_second, grad_out):
    kern_first = w_first.reshape(3, 3, 3, C_FULL, C_HALF)
    kern_second = w_second.reshape(3, 3, 3, C_HALF, C_HALF)
    flipped = kern_second[::-1, ::-1, ::-1]
    tile_ids = jnp.arange(N_TILE, dtype=jnp.int32)
    hits = (assign[:, :, None] == tile_ids[None, None, :]).astype(jnp.int32)
    inverse = lax.optimization_barrier(jnp.sum(hits * tile_ids[None, :, None], axis=1)).astype(jnp.int32)

    def step(carry, row):
        group = row // N_TILE
        slot = row % N_TILE
        scene_id = (group * N_TILE + inverse[group, slot]).astype(jnp.int32)
        source = lax.dynamic_index_in_dim(feats, scene_id, 0, keepdims=False)
        occ = lax.dynamic_index_in_dim(occupancy, scene_id, 0, keepdims=False)
        cot = lax.dynamic_index_in_dim(grad_out, row, 0, keepdims=False)
        full_mask = upsample(occ, BRICK).astype(jnp.bfloat16)
        half_mask = upsample(occ, BRICK // 2).astype(jnp.float32)[None, :, :, :, None]
        masked = (source.reshape(SX, SY, SZ, C_FULL) * full_mask[:, :, :, None])[None]
        pre = convolve(masked, kern_first, (2, 2, 2), [(1, 0), (1, 0), (1, 0)], 'DHWIO')
        hidden = (jax.nn.silu(pre) * half_mask).astype(jnp.bfloat16)
        second = convolve(hidden, kern_second, (1, 1, 1), [(1, 1), (1, 1), (1, 1)], 'DHWIO')
        decoded_row = (jax.nn.silu(second) * half_mask).astype(jnp.bfloat16)
        upstream = cot.reshape(1, HX, HY, HZ, C_HALF).astype(jnp.float32)
        d_second = (upstream * half_mask * silu_slope(second)).astype(jnp.bfloat16)
        hidden_pad = jnp.pad(hidden, ((0, 0), (1, 1), (1, 1), (1, 1), (0, 0)))
        part_second = kernel_grad(hidden_pad, d_second, 1)
        d_hidden = convolve(d_second, flipped, (1, 1, 1), [(1, 1), (1, 1), (1, 1)], 'DHWOI').astype(jnp.bfloat16)
        d_pre = (d_hidden.astype(jnp.float32) * half_mask * silu_slope(pre)).astype(jnp.bfloat16)
        masked_pad = jnp.pad(masked, ((0, 0), (1, 0), (1, 0), (1, 0), (0, 0)))
        part_first = kernel_grad(masked_pad, d_pre, 2)
        return ((carry[0] + part_first, carry[1] + part_second), decoded_row.reshape(HX, HY, HZ * C_HALF))
    start = (jnp.zeros((3, 3, 3, C_FULL, C_HALF), jnp.float32), jnp.zeros((3, 3, 3, C_HALF, C_HALF), jnp.float32))
    totals, decoded = lax.scan(step, start, jnp.arange(SCENES, dtype=jnp.int32))
    factor = 1.0 / math.sqrt(SCENES * HX * HY * HZ)
    grad_first = (totals[0] * factor).reshape(27 * C_FULL, C_HALF)
    grad_second = (totals[1] * factor).reshape(27 * C_HALF, C_HALF)
    return (decoded, grad_first, grad_second)
```

```python
import functools
import math

import jax
import jax.numpy as jnp
from jax import lax
from jax.experimental import pallas as pl
from jax.experimental.pallas import tpu as pltpu
from jax.sharding import PartitionSpec as P

MESH = pl.DeviceIdType.MESH
F32, BF16, I32 = jnp.float32, jnp.bfloat16, jnp.int32
SCENES, BX, SLOTS, NB = 16, 4, 2, 8
NONE = 16
TAPS = [(kx, ky) for kx in range(3) for ky in range(3)]
CHUNK = 48
VMEM_LIMIT = 60 * 1024 * 1024


def vmem():
    return pl.BlockSpec(memory_space=pltpu.VMEM)


def smem():
    return pl.BlockSpec(memory_space=pltpu.SMEM)


def pack_kernel(order_ref, code_ref, feats_ref, out_ref):
    @pl.loop(0, SCENES)
    def _(target):
        scene = order_ref[target]
        rows = []
        for slot in range(SLOTS):
            code = code_ref[target * SLOTS + slot]
            by = code // 4
            bz = code - 4 * by
            for plane in range(2):
                wide = feats_ref[scene, plane, :, pl.ds(pl.multiple_of(bz * 256, 256), 256)].astype(F32)
                acc = jnp.zeros((8, 256), F32)
                for k in range(4):
                    acc = jnp.where(by == k, wide[8 * k : 8 * k + 8], acc)
                rows.append(acc)
        out_ref[target] = jnp.concatenate(rows, axis=0).astype(BF16)


def pack(order, code, feats):
    return pl.pallas_call(
        pack_kernel,
        out_shape=jax.ShapeDtypeStruct((SCENES, 32, 256), BF16),
        in_specs=[smem(), smem(), vmem()],
        out_specs=vmem(),
        compiler_params=pltpu.CompilerParams(vmem_limit_bytes=VMEM_LIMIT),
        name="pack",
    )(order, code, feats)


def relayout_kernel(stage, out_ref, send_sem, recv_sem):
    me = lax.axis_index("tile")
    barrier = pltpu.get_barrier_semaphore()
    for step in range(1, SCENES):
        peer = lax.rem(me + step, SCENES)
        pl.semaphore_signal(barrier, inc=1, device_id={"tile": peer}, device_id_type=MESH)
    out_ref[me] = stage[me]
    pl.semaphore_wait(barrier, SCENES - 1)
    copies = []
    for step in range(1, SCENES):
        peer = lax.rem(me + step, SCENES)
        copy = pltpu.make_async_remote_copy(
            src_ref=stage.at[peer],
            dst_ref=out_ref.at[me],
            send_sem=send_sem.at[step],
            recv_sem=recv_sem.at[step],
            device_id={"tile": peer},
            device_id_type=MESH,
        )
        copy.start()
        copies.append(copy)
    for copy in copies:
        copy.wait_recv()
    for copy in copies:
        copy.wait_send()


def relayout(stage):
    return pl.pallas_call(
        relayout_kernel,
        out_shape=jax.ShapeDtypeStruct((SCENES, 32, 256), BF16),
        in_specs=[vmem()],
        out_specs=vmem(),
        scratch_shapes=[
            pltpu.SemaphoreType.DMA((SCENES,)),
            pltpu.SemaphoreType.DMA((SCENES,)),
        ],
        compiler_params=pltpu.CompilerParams(collective_id=0, has_side_effects=True, vmem_limit_bytes=VMEM_LIMIT),
        name="relayout",
    )(stage)


def iota(shape, dim):
    return lax.broadcasted_iota(I32, shape, dim)


def dot(lhs, rhs, dims=((1,), (0,))):
    return lax.dot_general(lhs, rhs, (dims, ((), ())), preferred_element_type=F32)


def sublane_gather(value, picker):
    index, hit = picker
    pieces = []
    for at in range(0, value.shape[1], 128):
        got = jnp.take_along_axis(value[:, at : at + 128], index, axis=0)
        pieces.append(jnp.where(hit, got, 0.0))
    return pieces[0] if len(pieces) == 1 else jnp.concatenate(pieces, axis=1)


def scene_kernel(code_ref, bricks_ref, w1_ref, w2_ref, w3_ref, cot_ref, dec_ref, pay_ref,
                 fe, he, de, wide1, wide2, wide3, p1, p2, p3):
    codes = [code_ref[b] for b in range(NB)]
    valid = [code < NONE for code in codes]
    bys = [code // 4 for code in codes]
    bzs = [code - 4 * by for code, by in zip(codes, bys)]
    place = [
        jnp.where(valid[b], (b // 2) * 64 + bys[b] * 8 + bzs[b], -10000 * (b + 1)) for b in range(NB)
    ]
    sub = iota((8, 128), 0)
    own = jnp.zeros((8, 128), I32)
    for b in range(NB):
        own = jnp.where(sub == b, place[b], own)

    def picker(dx, dy, dz):
        target = own + (dx * 64 + dy * 8 + dz)
        index = jnp.zeros((8, 128), I32)
        hit = sub < 0
        for b in range(NB):
            same = target == place[b]
            index = jnp.where(same, b, index)
            hit = hit | same
        return index, hit

    pick = {
        (dx, dy, dz): picker(dx, dy, dz)
        for dx in (-1, 0, 1) for dy in (-1, 0, 1) for dz in (-1, 0, 1) if (dx, dy, dz) != (0, 0, 0)
    }

    wide1[...] = jnp.zeros_like(wide1)
    wide2[...] = jnp.zeros_like(wide2)
    wide3[...] = jnp.zeros_like(wide3)
    for tap in range(9):
        base = tap * 384
        w = w1_ref[tap * 96 : tap * 96 + 96, :]
        wide1[base + 352 : base + 384, 0:64] = w[0:32]
        wide1[base : base + 64, 0:64] = w[32:96]
        for zo in range(1, 4):
            at = base + 32 * (2 * zo - 1)
            wide1[at : at + 96, 64 * zo : 64 * zo + 64] = w
        for source, target in ((w2_ref, wide2), (w3_ref, wide3)):
            w = source[tap * 192 : tap * 192 + 192, :]
            target[base + 320 : base + 384, 0:64] = w[0:64]
            target[base : base + 128, 0:64] = w[64:192]
            target[base : base + 192, 64:128] = w
            target[base + 64 : base + 256, 128:192] = w
            target[base + 128 : base + 256, 192:256] = w[0:128]
            target[base + 256 : base + 320, 192:256] = w[128:192]

    row, col = iota((128, 128), 0), iota((128, 128), 1)
    source = ((row // 2) % 4) * 32 + (row % 2) * 16 + (row // 64) * 8 + (row // 8) % 8
    perm = jnp.where(col == source, 1.0, 0.0).astype(BF16)
    for j in range(4):
        stack = jnp.concatenate([bricks_ref[4 * bx + j] for bx in range(BX)], axis=0)
        moved = dot(perm, stack).reshape(2, 8, 8, 256)
        for plane in range(2):
            fe[2 * j + plane + 1, 1:9, :, 0:256] = moved[plane]
    for px in range(-1, 8):
        for py in range(-1, 8):
            dx, dy = (-1 if px < 0 else 0), (-1 if py < 0 else 0)
            tile = fe[px % 8 + 1, py % 8 + 1, :, 0:256]
            if dx or dy:
                fe[px + 1, py + 1, :, 0:256] = sublane_gather(tile, pick[dx, dy, 0])
            fe[px + 1, py + 1, :, 256:384] = sublane_gather(tile[:, 128:256], pick[dx, dy, -1])
    for tap, (kx, ky) in enumerate(TAPS):
        rows = [fe[2 * x + kx, 2 * y + ky] for x in range(4) for y in range(4)]
        p1[:, tap * 384 : tap * 384 + 384] = jnp.concatenate(rows, axis=0).astype(BF16)
    pre = dot(p1[...], wide1[...])

    low = iota((8, 128), 1) < 64

    def extend(value, ext, patches):
        for x in range(4):
            for y in range(4):
                at = (x * 4 + y) * 8
                ext[x + 1, y + 1, :, 0:256] = value[at : at + 8]
        for px in range(-1, 5):
            for py in range(-1, 5):
                dx = -1 if px < 0 else (1 if px > 3 else 0)
                dy = -1 if py < 0 else (1 if py > 3 else 0)
                at = ((px % 4) * 4 + py % 4) * 8
                tile = value[at : at + 8]
                if dx or dy:
                    ext[px + 1, py + 1, :, 0:256] = sublane_gather(tile, pick[dx, dy, 0])
                above = sublane_gather(tile[:, 0:128], pick[dx, dy, 1])
                below = sublane_gather(tile[:, 128:256], pick[dx, dy, -1])
                ext[px + 1, py + 1, :, 256:384] = jnp.where(low, above, below)
        for tap, (kx, ky) in enumerate(TAPS):
            rows = [ext[x + kx, y + ky] for x in range(4) for y in range(4)]
            patches[:, tap * 384 : tap * 384 + 384] = jnp.concatenate(rows, axis=0).astype(BF16)

    sig_pre = jax.nn.sigmoid(pre)
    hidden = (pre * sig_pre).astype(BF16)
    extend(hidden.astype(F32), he, p2)
    second = dot(p2[...], wide2[...])
    sig = jax.nn.sigmoid(second)
    decoded = (second * sig).astype(BF16)

    row, col = iota((32, 128), 0), iota((32, 128), 1)
    goal = jnp.full((32, 128), -1, I32)
    row_t, col_t = iota((128, 32), 0), iota((128, 32), 1)
    goal_t = jnp.full((128, 32), -1, I32)
    for b in range(NB):
        start = jnp.where(valid[b], 16 * b + 4 * bys[b], -10000)
        goal = jnp.where(row % 8 == b, start + row // 8, goal)
        goal_t = jnp.where(col_t % 8 == b, start + col_t // 8, goal_t)
    take = jnp.where(col == goal, 1.0, 0.0).astype(BF16)
    give = jnp.where(row_t == goal_t, 1.0, 0.0).astype(BF16)
    ups = []
    for x in range(4):
        planes = []
        for b in range(NB):
            lane = pl.multiple_of(jnp.where(valid[b], bzs[b], 0) * 256, 256)
            planes.append(cot_ref[4 * (b // 2) + x, :, pl.ds(lane, 256)])
        ups.append(dot(take, jnp.concatenate(planes, axis=0)))
        spread = dot(give, decoded[32 * x : 32 * x + 32])
        for bx in range(BX):
            first, other = spread[32 * bx : 32 * bx + 16], spread[32 * bx + 16 : 32 * bx + 32]
            for c in range(4):
                block = jnp.where(bzs[2 * bx] == c, first, 0.0) + jnp.where(bzs[2 * bx + 1] == c, other, 0.0)
                dec_ref[4 * bx + x, :, 256 * c : 256 * c + 256] = block.astype(BF16)
    upstream = jnp.concatenate(ups, axis=0)

    d_second = (upstream * (sig * (1.0 + second * (1.0 - sig)))).astype(BF16)
    extend(d_second.astype(F32), de, p3)
    d_hidden = dot(p3[...], wide3[...]).astype(BF16)
    d_pre = (d_hidden.astype(F32) * (sig_pre * (1.0 + pre * (1.0 - sig_pre)))).astype(BF16)

    def fold(parts, target):
        half = parts[0].shape[0] // 2
        lo, hi = parts[0] + parts[2], parts[1] + parts[3]
        is_low = iota((half, 128), 1) < 64
        keep = jnp.where(is_low, lo[:half], hi[half:])
        turn = jnp.where(is_low, lo[half:], hi[:half])
        pay_ref[target : target + half, :] = keep + pltpu.roll(turn, 64, 1)

    for tap in range(9):
        full = dot(p1[:, tap * 384 : tap * 384 + 384], d_pre, ((0,), (0,)))
        parts = [jnp.concatenate([full[352:384, 0:128], full[0:64, 0:128]], axis=0)]
        for zo in range(1, 4):
            at, lane = 32 * (2 * zo - 1), 128 * (zo // 2)
            parts.append(full[at : at + 96, lane : lane + 128])
        fold(parts, tap * 48)
        full = dot(p2[:, tap * 384 : tap * 384 + 384], d_second, ((0,), (0,)))
        parts = [
            jnp.concatenate([full[320:384, 0:128], full[0:128, 0:128]], axis=0),
            full[0:192, 0:128],
            full[64:256, 128:256],
            full[128:320, 128:256],
        ]
        fold(parts, 432 + tap * 96)
    pay_ref[1296:1536, :] = jnp.zeros((240, 128), F32)


def scene_step(code, bricks, w1, w2, w3, cot):
    wide = pltpu.VMEM((3456, 256), BF16)
    patch = pltpu.VMEM((128, 3456), BF16)
    return pl.pallas_call(
        scene_kernel,
        out_shape=[
            jax.ShapeDtypeStruct((16, 16, 1024), BF16),
            jax.ShapeDtypeStruct((32 * CHUNK, 128), F32),
        ],
        in_specs=[smem()] + [vmem()] * 5,
        out_specs=[vmem(), vmem()],
        scratch_shapes=[
            pltpu.VMEM((9, 9, 8, 384), F32),
            pltpu.VMEM((6, 6, 8, 384), F32),
            pltpu.VMEM((6, 6, 8, 384), F32),
            wide, wide, wide, patch, patch, patch,
        ],
        compiler_params=pltpu.CompilerParams(vmem_limit_bytes=VMEM_LIMIT),
        name="scene_step",
    )(code, bricks, w1, w2, w3, cot)


def total_kernel(factor, pay_ref, out_ref, from_core, mine, from_scene, part, from_z,
                 core_send, core_recv, scene_send, scene_recv, z_send, z_recv,
                 out_send, out_recv, back_send, back_recv):
    tile, scene = lax.axis_index("tile"), lax.axis_index("scene")
    core = lax.rem(tile, 2)
    z = tile // 2
    sibling = 2 * z + 1 - core

    def to_core():
        return {"tile": sibling}

    def to_scene(peer):
        return {"scene": peer}

    def to_z(peer):
        return {"tile": 2 * peer + core}

    barrier = pltpu.get_barrier_semaphore()
    pl.semaphore_signal(barrier, inc=1, device_id=to_core(), device_id_type=MESH)
    for step in range(1, 16):
        pl.semaphore_signal(barrier, inc=1, device_id=to_scene(lax.rem(scene + step, 16)), device_id_type=MESH)
    for step in range(1, 8):
        pl.semaphore_signal(barrier, inc=1, device_id=to_z(lax.rem(z + step, 8)), device_id_type=MESH)
    pl.semaphore_wait(barrier, 23)

    def remote(src, dst, send, recv, device):
        return pltpu.make_async_remote_copy(
            src_ref=src, dst_ref=dst, send_sem=send, recv_sem=recv, device_id=device, device_id_type=MESH
        )

    waits = []
    cores = []
    for step in range(16):
        owner = lax.rem(scene + step, 16)
        copy = remote(
            pay_ref.at[1 - core, owner], from_core.at[owner], core_send.at[step], core_recv.at[step], to_core()
        )
        copy.start()
        cores.append(copy)
    waits += cores
    scenes = []
    for step in list(range(1, 16)) + [0]:
        owner = lax.rem(scene + step, 16)
        cores[step].wait_recv()
        added = pay_ref[core, owner] + from_core[owner]
        if step == 0:
            from_scene[scene] = added
            continue
        mine[owner] = added
        copy = remote(
            mine.at[owner], from_scene.at[scene], scene_send.at[step], scene_recv.at[step], to_scene(owner)
        )
        copy.start()
        scenes.append(copy)
    waits += scenes
    for copy in scenes:
        copy.wait_recv()
    total = from_scene[0]
    for k in range(1, 16):
        total = total + from_scene[k]
    part[...] = total
    from_z[z] = total
    zs = []
    for step in range(1, 8):
        copy = remote(
            part, from_z.at[z], z_send.at[step], z_recv.at[step], to_z(lax.rem(z + step, 8))
        )
        copy.start()
        zs.append(copy)
    waits += zs
    for copy in zs:
        copy.wait_recv()
    total = from_z[0]
    for k in range(1, 8):
        total = total + from_z[k]
    out_ref[core, scene] = total * factor
    outs = [None]
    backs = []
    for step in range(1, 16):
        copy = remote(
            out_ref.at[core, scene], out_ref.at[core, scene], out_send.at[step], out_recv.at[step],
            to_scene(lax.rem(scene + step, 16)),
        )
        copy.start()
        outs.append(copy)
    for step in range(16):
        owner = lax.rem(scene - step + 16, 16)
        if step:
            outs[step].wait_recv()
        copy = remote(
            out_ref.at[core, owner], out_ref.at[core, owner], back_send.at[step], back_recv.at[step], to_core()
        )
        copy.start()
        backs.append(copy)
    for copy in backs:
        copy.wait_recv()
    for copy in waits + outs[1:] + backs:
        copy.wait_send()


def total_over_devices(payload, factor):
    sem = lambda n: pltpu.SemaphoreType.DMA((n,))
    return pl.pallas_call(
        functools.partial(total_kernel, factor),
        out_shape=jax.ShapeDtypeStruct((2, 16, CHUNK, 128), F32),
        in_specs=[vmem()],
        out_specs=vmem(),
        scratch_shapes=[
            pltpu.VMEM((16, CHUNK, 128), F32),
            pltpu.VMEM((16, CHUNK, 128), F32),
            pltpu.VMEM((16, CHUNK, 128), F32),
            pltpu.VMEM((CHUNK, 128), F32),
            pltpu.VMEM((8, CHUNK, 128), F32),
            sem(16), sem(16), sem(16), sem(16), sem(8), sem(8), sem(16), sem(16), sem(16), sem(16),
        ],
        compiler_params=pltpu.CompilerParams(collective_id=1, has_side_effects=True, vmem_limit_bytes=VMEM_LIMIT),
        name="total_over_devices",
    )(payload.reshape(2, 16, CHUNK, 128))


def brick_codes(occupancy):
    flags = occupancy.reshape(occupancy.shape[0], BX, 16) > 0
    ids = jnp.arange(16, dtype=I32)
    first = jnp.min(jnp.where(flags, ids, NONE), axis=-1)
    last = jnp.max(jnp.where(flags, ids, -1), axis=-1)
    return jnp.stack([first, jnp.where(last > first, last, NONE)], axis=-1)


def unpack(payload, taps, rows):
    return payload.reshape(taps, rows // 2, 2, 64).transpose(0, 2, 1, 3).reshape(taps * rows, 64)


def per_device(feats, occupancy, assign, w_first, w_second, grad_out):
    tile = lax.axis_index("tile")
    tile_ids = jnp.arange(SCENES, dtype=I32)
    hits = (assign[0][:, None] == tile_ids[None, :]).astype(I32)
    order = jnp.sum(hits * tile_ids[:, None], axis=0)
    codes = brick_codes(occupancy)
    at_row = lax.dynamic_index_in_dim(codes, tile // 4, 1, keepdims=False)
    code = jnp.sum(hits[:, :, None] * at_row[:, None, :], axis=0).reshape(SCENES * SLOTS)
    own_hit = (assign[0] == tile).astype(I32)
    own_code = jnp.sum(own_hit[:, None] * codes.reshape(SCENES, NB), axis=0)
    bricks = relayout(pack(order, code, feats))
    w3 = w_second.reshape(27, 64, 64)[::-1].transpose(0, 2, 1).reshape(27 * 64, 64)
    decoded, payload = scene_step(own_code, bricks, w_first, w_second, w3, grad_out[0])
    factor = 1.0 / math.sqrt(256 * 16 * 16 * 16)
    total = total_over_devices(payload, factor).reshape(32 * CHUNK, 128)
    grad_first = unpack(total[0:432], 9, 96)
    grad_second = unpack(total[432:1296], 9, 192)
    return decoded[None], grad_first, grad_second


def solution(mesh):
    return jax.shard_map(
        per_device,
        mesh=mesh,
        in_specs=(
            P("scene", "tile", None, None),
            P("scene", None, None, None),
            P("scene", None),
            P(),
            P(),
            P(("scene", "tile"), None, None, None),
        ),
        out_specs=(P(("scene", "tile"), None, None, None), P(), P()),
        check_vma=False,
    )
```

```python
import functools
import math

import jax
import jax.numpy as jnp
from jax import lax
from jax.experimental import pallas as pl
from jax.experimental.pallas import tpu as pltpu
from jax.sharding import PartitionSpec as P

MESH = pl.DeviceIdType.MESH
F32, BF16, I32 = jnp.float32, jnp.bfloat16, jnp.int32
SCENES, BX, SLOTS, NB = 16, 4, 2, 8
NONE = 16
TAPS = [(kx, ky) for kx in range(3) for ky in range(3)]
CHUNK = 48
VMEM_LIMIT = 60 * 1024 * 1024


def vmem():
    return pl.BlockSpec(memory_space=pltpu.VMEM)


def smem():
    return pl.BlockSpec(memory_space=pltpu.SMEM)


def iota(shape, dim):
    return lax.broadcasted_iota(I32, shape, dim)


def row_codes(planes):
    first, last = NONE, -1
    for by in range(4):
        flags = planes[by] > 0
        ids = iota(planes[by].shape, 0) + 4 * by
        first = jnp.minimum(first, jnp.where(flags, ids, NONE))
        last = jnp.maximum(last, jnp.where(flags, ids, -1))
    first = jnp.min(first.astype(F32), axis=0, keepdims=True).astype(I32)
    last = jnp.max(last.astype(F32), axis=0, keepdims=True).astype(I32)
    return first, jnp.where(last > first, last, NONE)


def relayout_kernel(assign_ref, owner_ref, occ_ref, feats_ref, out_ref, own_ref, packed, stage, send_sem, recv_sem):
    me = lax.axis_index("tile")
    barrier = pltpu.get_barrier_semaphore()
    for step in range(1, SCENES):
        peer = lax.rem(me + step, SCENES)
        pl.semaphore_signal(barrier, inc=1, device_id={"tile": peer}, device_id_type=MESH)

    here = me // 4
    slots = row_codes([occ_ref[here, by] for by in range(4)])
    for scene in range(SCENES):
        marks = [jnp.broadcast_to(code[:, scene : scene + 1], (8, 256)) for code in slots]
        bys = [mark // 4 for mark in marks]
        bzs = [mark % 4 for mark in marks]
        rows = [[None, None], [None, None]]
        for plane in range(2):
            wide = feats_ref[scene, plane].astype(F32)
            for slot in range(SLOTS):
                acc = jnp.zeros((8, 256), F32)
                for by in range(4):
                    line = wide[8 * by : 8 * by + 8]
                    part = line[:, 0:256]
                    for bz in range(1, 4):
                        part = jnp.where(bzs[slot] == bz, line[:, 256 * bz : 256 * bz + 256], part)
                    acc = jnp.where(bys[slot] == by, part, acc)
                rows[slot][plane] = acc
        packed[scene] = jnp.concatenate(rows[0] + rows[1], axis=0).astype(BF16)

    def scene_of(target):
        scene = 0
        for j in range(SCENES):
            scene = jnp.where(assign_ref[0, j] == target, j, scene)
        return scene

    out_ref[me] = packed[scene_of(me)]
    pl.semaphore_wait(barrier, SCENES - 1)
    copies = []
    for step in range(1, SCENES):
        peer = lax.rem(me + step, SCENES)
        stage[peer] = packed[scene_of(peer)]
        copy = pltpu.make_async_remote_copy(
            src_ref=stage.at[peer],
            dst_ref=out_ref.at[me],
            send_sem=send_sem.at[step],
            recv_sem=recv_sem.at[step],
            device_id={"tile": peer},
            device_id_type=MESH,
        )
        copy.start()
        copies.append(copy)
    codes = []
    for bx in range(BX):
        codes += row_codes([occ_ref[bx, by] for by in range(4)])
    mine = jnp.where(owner_ref[...] == me, jnp.concatenate(codes, axis=0), 0)
    own = jnp.sum(mine.astype(F32), axis=1, keepdims=True).astype(I32)
    own_ref[...] = jnp.broadcast_to(own, (NB, 128))
    for copy in copies:
        copy.wait_recv()
    for copy in copies:
        copy.wait_send()


def relayout(assign, occupancy, feats):
    return pl.pallas_call(
        relayout_kernel,
        out_shape=[
            jax.ShapeDtypeStruct((SCENES, 32, 256), BF16),
            jax.ShapeDtypeStruct((NB, 128), I32),
        ],
        in_specs=[smem(), vmem(), vmem(), vmem()],
        out_specs=[vmem(), vmem()],
        scratch_shapes=[
            pltpu.VMEM((SCENES, 32, 256), BF16),
            pltpu.VMEM((SCENES, 32, 256), BF16),
            pltpu.SemaphoreType.DMA((SCENES,)),
            pltpu.SemaphoreType.DMA((SCENES,)),
        ],
        compiler_params=pltpu.CompilerParams(collective_id=0, has_side_effects=True, vmem_limit_bytes=VMEM_LIMIT),
        name="relayout",
    )(assign, assign, occupancy.transpose(1, 2, 3, 0), feats)


def dot(lhs, rhs, dims=((1,), (0,))):
    return lax.dot_general(lhs, rhs, (dims, ((), ())), preferred_element_type=F32)


def sublane_gather(value, picker):
    index, hit = picker
    pieces = []
    for at in range(0, value.shape[1], 128):
        got = jnp.take_along_axis(value[:, at : at + 128], index, axis=0)
        pieces.append(jnp.where(hit, got, 0.0))
    return pieces[0] if len(pieces) == 1 else jnp.concatenate(pieces, axis=1)


def scene_kernel(code_ref, bricks_ref, w1_ref, w2_ref, cot_ref, dec_ref, pay_ref,
                 fe, he, de, wide1, wide2, wide3, p1, p2, p3):
    codes = [code_ref[b, 0] for b in range(NB)]
    valid = [code < NONE for code in codes]
    bys = [code // 4 for code in codes]
    bzs = [code - 4 * by for code, by in zip(codes, bys)]
    place = [
        jnp.where(valid[b], (b // 2) * 64 + bys[b] * 8 + bzs[b], -10000 * (b + 1)) for b in range(NB)
    ]
    sub = iota((8, 128), 0)
    own = jnp.zeros((8, 128), I32)
    for b in range(NB):
        own = jnp.where(sub == b, place[b], own)

    def picker(dx, dy, dz):
        target = own + (dx * 64 + dy * 8 + dz)
        index = jnp.zeros((8, 128), I32)
        hit = sub < 0
        for b in range(NB):
            same = target == place[b]
            index = jnp.where(same, b, index)
            hit = hit | same
        return index, hit

    pick = {
        (dx, dy, dz): picker(dx, dy, dz)
        for dx in (-1, 0, 1) for dy in (-1, 0, 1) for dz in (-1, 0, 1) if (dx, dy, dz) != (0, 0, 0)
    }

    wide1[...] = jnp.zeros_like(wide1)
    wide2[...] = jnp.zeros_like(wide2)
    wide3[...] = jnp.zeros_like(wide3)
    def turned(ref):
        return ref[...].astype(F32).T.astype(BF16)

    first, second = turned(w1_ref), turned(w2_ref)
    for tap in range(9):
        base = tap * 384
        w = first[tap * 96 : tap * 96 + 96]
        wide1[base + 352 : base + 384, 0:64] = w[0:32]
        wide1[base : base + 64, 0:64] = w[32:96]
        for zo in range(1, 4):
            at = base + 32 * (2 * zo - 1)
            wide1[at : at + 96, 64 * zo : 64 * zo + 64] = w
        forward = [second[(3 * tap + kz) * 64 : (3 * tap + kz) * 64 + 64] for kz in range(3)]
        backward = [w2_ref[:, (26 - 3 * tap - kz) * 64 : (26 - 3 * tap - kz) * 64 + 64] for kz in range(3)]
        for target, blocks in ((wide2, forward), (wide3, backward)):
            for zo in range(4):
                for kz in range(3):
                    zi = zo + kz - 1
                    at = base + (320 if zi < 0 else 64 * zi)
                    target[at : at + 64, 64 * zo : 64 * zo + 64] = blocks[kz]

    row, col = iota((128, 128), 0), iota((128, 128), 1)
    source = ((row // 2) % 4) * 32 + (row % 2) * 16 + (row // 64) * 8 + (row // 8) % 8
    perm = jnp.where(col == source, 1.0, 0.0).astype(BF16)
    for j in range(4):
        stack = jnp.concatenate([bricks_ref[4 * bx + j] for bx in range(BX)], axis=0)
        moved = dot(perm, stack).reshape(2, 8, 8, 256)
        for plane in range(2):
            fe[2 * j + plane + 1, 1:9, :, 0:256] = moved[plane]
    for px in range(-1, 8):
        for py in range(-1, 8):
            dx, dy = (-1 if px < 0 else 0), (-1 if py < 0 else 0)
            tile = fe[px % 8 + 1, py % 8 + 1, :, 0:256]
            if dx or dy:
                fe[px + 1, py + 1, :, 0:256] = sublane_gather(tile, pick[dx, dy, 0])
            fe[px + 1, py + 1, :, 256:384] = sublane_gather(tile[:, 128:256], pick[dx, dy, -1])
    for tap, (kx, ky) in enumerate(TAPS):
        rows = [fe[2 * x + kx, 2 * y + ky] for x in range(4) for y in range(4)]
        p1[:, tap * 384 : tap * 384 + 384] = jnp.concatenate(rows, axis=0).astype(BF16)
    pre = dot(p1[...], wide1[...])

    low = iota((8, 128), 1) < 64

    def extend(value, ext, patches):
        for x in range(4):
            for y in range(4):
                at = (x * 4 + y) * 8
                ext[x + 1, y + 1, :, 0:256] = value[at : at + 8]
        for px in range(-1, 5):
            for py in range(-1, 5):
                dx = -1 if px < 0 else (1 if px > 3 else 0)
                dy = -1 if py < 0 else (1 if py > 3 else 0)
                at = ((px % 4) * 4 + py % 4) * 8
                tile = value[at : at + 8]
                if dx or dy:
                    ext[px + 1, py + 1, :, 0:256] = sublane_gather(tile, pick[dx, dy, 0])
                above = sublane_gather(tile[:, 0:128], pick[dx, dy, 1])
                below = sublane_gather(tile[:, 128:256], pick[dx, dy, -1])
                ext[px + 1, py + 1, :, 256:384] = jnp.where(low, above, below)
        for tap, (kx, ky) in enumerate(TAPS):
            rows = [ext[x + kx, y + ky] for x in range(4) for y in range(4)]
            patches[:, tap * 384 : tap * 384 + 384] = jnp.concatenate(rows, axis=0).astype(BF16)

    sig_pre = jax.nn.sigmoid(pre)
    hidden = (pre * sig_pre).astype(BF16)
    extend(hidden.astype(F32), he, p2)
    second = dot(p2[...], wide2[...])
    sig = jax.nn.sigmoid(second)
    decoded = (second * sig).astype(BF16)

    row, col = iota((32, 128), 0), iota((32, 128), 1)
    goal = jnp.full((32, 128), -1, I32)
    row_t, col_t = iota((128, 32), 0), iota((128, 32), 1)
    goal_t = jnp.full((128, 32), -1, I32)
    for b in range(NB):
        start = jnp.where(valid[b], 16 * b + 4 * bys[b], -10000)
        goal = jnp.where(row % 8 == b, start + row // 8, goal)
        goal_t = jnp.where(col_t % 8 == b, start + col_t // 8, goal_t)
    take = jnp.where(col == goal, 1.0, 0.0).astype(BF16)
    give = jnp.where(row_t == goal_t, 1.0, 0.0).astype(BF16)
    ups = []
    for x in range(4):
        planes = []
        for b in range(NB):
            lane = pl.multiple_of(jnp.where(valid[b], bzs[b], 0) * 256, 256)
            planes.append(cot_ref[4 * (b // 2) + x, :, pl.ds(lane, 256)])
        ups.append(dot(take, jnp.concatenate(planes, axis=0)))
        spread = dot(give, decoded[32 * x : 32 * x + 32])
        for bx in range(BX):
            first, other = spread[32 * bx : 32 * bx + 16], spread[32 * bx + 16 : 32 * bx + 32]
            for c in range(4):
                block = jnp.where(bzs[2 * bx] == c, first, 0.0) + jnp.where(bzs[2 * bx + 1] == c, other, 0.0)
                dec_ref[4 * bx + x, :, 256 * c : 256 * c + 256] = block.astype(BF16)
    upstream = jnp.concatenate(ups, axis=0)

    d_second = (upstream * (sig * (1.0 + second * (1.0 - sig)))).astype(BF16)
    extend(d_second.astype(F32), de, p3)
    d_hidden = dot(p3[...], wide3[...]).astype(BF16)
    d_pre = (d_hidden.astype(F32) * (sig_pre * (1.0 + pre * (1.0 - sig_pre)))).astype(BF16)

    def halves(parts):
        size = parts[0].shape[0] // 2
        lo, hi = parts[0] + parts[2], parts[1] + parts[3]
        return [(lo[:size], hi[:size]), (lo[size:], hi[size:])]

    def fold(lower, upper, target):
        size = lower[0].shape[0]
        is_low = iota((size, 128), 1) < 64
        keep = jnp.where(is_low, lower[0], upper[1])
        turn = jnp.where(is_low, upper[0], lower[1])
        pay_ref[target : target + size, :] = keep + pltpu.roll(turn, 64, 1)

    blocks1, blocks2 = [], []
    for tap in range(9):
        full = dot(p2[:, tap * 384 : tap * 384 + 384], d_second, ((0,), (0,)))
        blocks2 += halves([
            jnp.concatenate([full[320:384, 0:128], full[0:128, 0:128]], axis=0),
            full[0:192, 0:128],
            full[64:256, 128:256],
            full[128:320, 128:256],
        ])
    for at in range(9):
        fold(blocks2[at], blocks2[at + 9], 432 + at * 96)
    for tap in range(9):
        full = dot(p1[:, tap * 384 : tap * 384 + 384], d_pre, ((0,), (0,)))
        parts = [jnp.concatenate([full[352:384, 0:128], full[0:64, 0:128]], axis=0)]
        for zo in range(1, 4):
            at, lane = 32 * (2 * zo - 1), 128 * (zo // 2)
            parts.append(full[at : at + 96, lane : lane + 128])
        blocks1 += halves(parts)
    for at in range(9):
        fold(blocks1[at], blocks1[at + 9], at * 48)
    pay_ref[1296:1536, :] = jnp.zeros((240, 128), F32)


def scene_step(code, bricks, w1, w2, cot):
    wide = pltpu.VMEM((3456, 256), BF16)
    patch = pltpu.VMEM((128, 3456), BF16)
    return pl.pallas_call(
        scene_kernel,
        out_shape=[
            jax.ShapeDtypeStruct((16, 16, 1024), BF16),
            jax.ShapeDtypeStruct((32 * CHUNK, 128), F32),
        ],
        in_specs=[smem()] + [vmem()] * 4,
        out_specs=[vmem(), vmem()],
        scratch_shapes=[
            pltpu.VMEM((9, 9, 8, 384), F32),
            pltpu.VMEM((6, 6, 8, 384), F32),
            pltpu.VMEM((6, 6, 8, 384), F32),
            wide, wide, wide, patch, patch, patch,
        ],
        compiler_params=pltpu.CompilerParams(vmem_limit_bytes=VMEM_LIMIT),
        name="scene_step",
    )(code, bricks, w1, w2, cot)


def total_kernel(factor, pay_ref, out_ref, from_core, mine, from_scene, part, from_z,
                 core_send, core_recv, scene_send, scene_recv, z_send, z_recv,
                 out_send, out_recv, back_send, back_recv):
    tile, scene = lax.axis_index("tile"), lax.axis_index("scene")
    core = lax.rem(tile, 2)
    z = tile // 2
    sibling = 2 * z + 1 - core

    def to_core():
        return {"tile": sibling}

    def to_scene(peer):
        return {"scene": peer}

    def to_z(peer):
        return {"tile": 2 * peer + core}

    barrier = pltpu.get_barrier_semaphore()
    pl.semaphore_signal(barrier, inc=1, device_id=to_core(), device_id_type=MESH)
    for step in range(1, 16):
        pl.semaphore_signal(barrier, inc=1, device_id=to_scene(lax.rem(scene + step, 16)), device_id_type=MESH)
    for step in range(1, 8):
        pl.semaphore_signal(barrier, inc=1, device_id=to_z(lax.rem(z + step, 8)), device_id_type=MESH)
    pl.semaphore_wait(barrier, 23)

    def remote(src, dst, send, recv, device):
        return pltpu.make_async_remote_copy(
            src_ref=src, dst_ref=dst, send_sem=send, recv_sem=recv, device_id=device, device_id_type=MESH
        )

    waits = []
    cores = []
    for step in range(16):
        owner = lax.rem(scene + step, 16)
        copy = remote(
            pay_ref.at[1 - core, owner], from_core.at[owner], core_send.at[step], core_recv.at[step], to_core()
        )
        copy.start()
        cores.append(copy)
    waits += cores
    scenes = []
    for step in list(range(1, 16)) + [0]:
        owner = lax.rem(scene + step, 16)
        cores[step].wait_recv()
        added = pay_ref[core, owner] + from_core[owner]
        if step == 0:
            from_scene[scene] = added.astype(BF16)
            continue
        mine[owner] = added.astype(BF16)
        copy = remote(
            mine.at[owner], from_scene.at[scene], scene_send.at[step], scene_recv.at[step], to_scene(owner)
        )
        copy.start()
        scenes.append(copy)
    waits += scenes
    for copy in scenes:
        copy.wait_recv()
    total = from_scene[0].astype(F32)
    for k in range(1, 16):
        total = total + from_scene[k].astype(F32)
    part[...] = total.astype(BF16)
    from_z[z] = total.astype(BF16)
    zs = []
    for step in range(1, 8):
        copy = remote(
            part, from_z.at[z], z_send.at[step], z_recv.at[step], to_z(lax.rem(z + step, 8))
        )
        copy.start()
        zs.append(copy)
    waits += zs
    for copy in zs:
        copy.wait_recv()
    total = from_z[0].astype(F32)
    for k in range(1, 8):
        total = total + from_z[k].astype(F32)
    out_ref[core, scene] = (total * factor).astype(BF16)
    outs = [None]
    backs = []
    for step in range(1, 16):
        copy = remote(
            out_ref.at[core, scene], out_ref.at[core, scene], out_send.at[step], out_recv.at[step],
            to_scene(lax.rem(scene + step, 16)),
        )
        copy.start()
        outs.append(copy)
    for step in range(16):
        owner = lax.rem(scene - step + 16, 16)
        if step:
            outs[step].wait_recv()
        copy = remote(
            out_ref.at[core, owner], out_ref.at[core, owner], back_send.at[step], back_recv.at[step], to_core()
        )
        copy.start()
        backs.append(copy)
    for copy in backs:
        copy.wait_recv()
    for copy in waits + outs[1:] + backs:
        copy.wait_send()


def total_over_devices(payload, factor):
    sem = lambda n: pltpu.SemaphoreType.DMA((n,))
    return pl.pallas_call(
        functools.partial(total_kernel, factor),
        out_shape=jax.ShapeDtypeStruct((2, 16, CHUNK, 128), BF16),
        in_specs=[vmem()],
        out_specs=vmem(),
        scratch_shapes=[
            pltpu.VMEM((16, CHUNK, 128), F32),
            pltpu.VMEM((16, CHUNK, 128), BF16),
            pltpu.VMEM((16, CHUNK, 128), BF16),
            pltpu.VMEM((CHUNK, 128), BF16),
            pltpu.VMEM((8, CHUNK, 128), BF16),
            sem(16), sem(16), sem(16), sem(16), sem(8), sem(8), sem(16), sem(16), sem(16), sem(16),
        ],
        compiler_params=pltpu.CompilerParams(collective_id=1, has_side_effects=True, vmem_limit_bytes=VMEM_LIMIT),
        name="total_over_devices",
    )(payload.reshape(2, 16, CHUNK, 128))


def unpack_kernel(total_ref, first_ref, second_ref):
    row, col = iota((64, 128), 0), iota((64, 128), 1)
    for half in range(2):
        pick = jnp.where(col == row + 64 * half, 1.0, 0.0).astype(BF16)
        first_ref[:, 432 * half : 432 * half + 432] = dot(pick, total_ref[0:432], ((1,), (1,)))
        second_ref[:, 864 * half : 864 * half + 864] = dot(pick, total_ref[432:1296], ((1,), (1,)))


def unpack(total):
    return pl.pallas_call(
        unpack_kernel,
        out_shape=[jax.ShapeDtypeStruct((64, 864), F32), jax.ShapeDtypeStruct((64, 1728), F32)],
        in_specs=[vmem()],
        out_specs=[vmem(), vmem()],
        compiler_params=pltpu.CompilerParams(vmem_limit_bytes=VMEM_LIMIT),
        name="unpack",
    )(total)


def per_device(feats, occupancy, assign, w_first, w_second, grad_out):
    bricks, own_code = relayout(assign, occupancy, feats)
    decoded, payload = scene_step(own_code, bricks, w_first.T, w_second.T, grad_out[0])
    factor = 1.0 / math.sqrt(256 * 16 * 16 * 16)
    total = total_over_devices(payload, factor)
    grad_first, grad_second = unpack(total.reshape(32 * CHUNK, 128))
    return decoded[None], grad_first.T, grad_second.T


def solution(mesh):
    return jax.shard_map(
        per_device,
        mesh=mesh,
        in_specs=(
            P("scene", "tile", None, None),
            P("scene", None, None, None),
            P("scene", None),
            P(),
            P(),
            P(("scene", "tile"), None, None, None),
        ),
        out_specs=(P(("scene", "tile"), None, None, None), P(), P()),
        check_vma=False,
    )
```

```python
import functools
import math

import jax
import jax.numpy as jnp
from jax import lax
from jax.experimental import pallas as pl
from jax.experimental.pallas import tpu as pltpu
from jax.sharding import PartitionSpec as P

MESH = pl.DeviceIdType.MESH
F32, BF16, I32 = jnp.float32, jnp.bfloat16, jnp.int32
SCENES, BX, SLOTS, NB = 16, 4, 2, 8
NONE = 16
TAPS = [(kx, ky) for kx in range(3) for ky in range(3)]
CHUNK = 48
VMEM_LIMIT = 60 * 1024 * 1024


def vmem():
    return pl.BlockSpec(memory_space=pltpu.VMEM)


def smem():
    return pl.BlockSpec(memory_space=pltpu.SMEM)


def iota(shape, dim):
    return lax.broadcasted_iota(I32, shape, dim)


def dot(lhs, rhs, dims=((1,), (0,))):
    return lax.dot_general(lhs, rhs, (dims, ((), ())), preferred_element_type=F32)


def remote(src, dst, send, recv, device):
    return pltpu.make_async_remote_copy(
        src_ref=src, dst_ref=dst, send_sem=send, recv_sem=recv, device_id=device, device_id_type=MESH
    )


def row_codes(planes):
    first, last = NONE, -1
    for by in range(4):
        flags = planes[by] > 0
        ids = iota(planes[by].shape, 0) + 4 * by
        first = jnp.minimum(first, jnp.where(flags, ids, NONE))
        last = jnp.maximum(last, jnp.where(flags, ids, -1))
    first = jnp.min(first.astype(F32), axis=0, keepdims=True).astype(I32)
    last = jnp.max(last.astype(F32), axis=0, keepdims=True).astype(I32)
    return first, jnp.where(last > first, last, NONE)


def pack_scene(feats_ref, scene, slots, packed):
    marks = [jnp.broadcast_to(code[:, scene : scene + 1], (8, 256)) for code in slots]
    bys = [mark // 4 for mark in marks]
    bzs = [mark % 4 for mark in marks]
    rows = [[None, None], [None, None]]
    for plane in range(2):
        wide = feats_ref[scene, plane].astype(F32)
        for slot in range(SLOTS):
            acc = jnp.zeros((8, 256), F32)
            for by in range(4):
                line = wide[8 * by : 8 * by + 8]
                part = line[:, 0:256]
                for bz in range(1, 4):
                    part = jnp.where(bzs[slot] == bz, line[:, 256 * bz : 256 * bz + 256], part)
                acc = jnp.where(bys[slot] == by, part, acc)
            rows[slot][plane] = acc
    packed[scene] = jnp.concatenate(rows[0] + rows[1], axis=0).astype(BF16)


def scene_of(assign_ref, target):
    scene = 0
    for j in range(SCENES):
        scene = jnp.where(assign_ref[0, j] == target, j, scene)
    return scene


def own_codes(occ_ref, owner, me):
    codes = []
    for bx in range(BX):
        codes += row_codes([occ_ref[bx, by] for by in range(4)])
    mine = jnp.where(owner == me, jnp.concatenate(codes, axis=0), 0)
    own = jnp.sum(mine.astype(F32), axis=1, keepdims=True).astype(I32)
    return jnp.broadcast_to(own, (NB, 128))


def sublane_gather(value, picker):
    index, hit = picker
    pieces = []
    for at in range(0, value.shape[1], 128):
        got = jnp.take_along_axis(value[:, at : at + 128], index, axis=0)
        pieces.append(jnp.where(hit, got, 0.0))
    return pieces[0] if len(pieces) == 1 else jnp.concatenate(pieces, axis=1)


def pickers(own):
    sub = iota((NB, 128), 0)
    place = jnp.where(own < NONE, (sub // 2) * 64 + (own // 4) * 8 + own % 4, -10000 * (sub + 1))
    each = [jnp.broadcast_to(place[b : b + 1], (NB, 128)) for b in range(NB)]
    pick = {}
    for dx in (-1, 0, 1):
        for dy in (-1, 0, 1):
            for dz in (-1, 0, 1):
                if (dx, dy, dz) == (0, 0, 0):
                    continue
                target = place + (dx * 64 + dy * 8 + dz)
                index = jnp.zeros((NB, 128), I32)
                hit = jnp.zeros((NB, 128), I32)
                for b in range(NB):
                    same = target == each[b]
                    index = jnp.where(same, b, index)
                    hit = jnp.where(same, 1, hit)
                pick[dx, dy, dz] = index, hit > 0
    return pick


def banded(w1_ref, w2_ref, wide1, wide2, wide3):
    wide1[...] = jnp.zeros_like(wide1)
    wide2[...] = jnp.zeros_like(wide2)
    wide3[...] = jnp.zeros_like(wide3)

    def turned(ref):
        return ref[...].astype(F32).T.astype(BF16)

    first, second = turned(w1_ref), turned(w2_ref)
    for tap in range(9):
        base = tap * 384
        w = first[tap * 96 : tap * 96 + 96]
        wide1[base + 352 : base + 384, 0:64] = w[0:32]
        wide1[base : base + 64, 0:64] = w[32:96]
        for zo in range(1, 4):
            at = base + 32 * (2 * zo - 1)
            wide1[at : at + 96, 64 * zo : 64 * zo + 64] = w
        forward = [second[(3 * tap + kz) * 64 : (3 * tap + kz) * 64 + 64] for kz in range(3)]
        backward = [w2_ref[:, (26 - 3 * tap - kz) * 64 : (26 - 3 * tap - kz) * 64 + 64] for kz in range(3)]
        for target, blocks in ((wide2, forward), (wide3, backward)):
            for zo in range(4):
                for kz in range(3):
                    zi = zo + kz - 1
                    at = base + (320 if zi < 0 else 64 * zi)
                    target[at : at + 64, 64 * zo : 64 * zo + 64] = blocks[kz]


def upstream_bricks(own, cot_ref):
    row, col = iota((32, 128), 0), iota((32, 128), 1)
    start = jnp.where(own < NONE, iota((NB, 128), 0) * 16 + (own // 4) * 4, -10000)
    goal = jnp.concatenate([start] * 4, axis=0) + row // 8
    take = jnp.where(col == goal, 1.0, 0.0).astype(BF16)
    bzs = own % 4
    marks = [jnp.broadcast_to(bzs[b : b + 1, 0:1], (16, 256)) for b in range(NB)]
    ups = []
    for x in range(4):
        planes = []
        for bx in range(BX):
            wide = cot_ref[4 * bx + x].astype(F32)
            for slot in range(SLOTS):
                part = wide[:, 0:256]
                for bz in range(1, 4):
                    part = jnp.where(marks[2 * bx + slot] == bz, wide[:, 256 * bz : 256 * bz + 256], part)
                planes.append(part)
        ups.append(dot(take, jnp.concatenate(planes, axis=0).astype(BF16)))
    return jnp.concatenate(ups, axis=0)


def first_patches(pick, bricks_ref, fe, p1):
    row, col = iota((128, 128), 0), iota((128, 128), 1)
    source = ((row // 2) % 4) * 32 + (row % 2) * 16 + (row // 64) * 8 + (row // 8) % 8
    perm = jnp.where(col == source, 1.0, 0.0).astype(BF16)
    for j in range(4):
        stack = jnp.concatenate([bricks_ref[4 * bx + j] for bx in range(BX)], axis=0)
        moved = dot(perm, stack).reshape(2, 8, 8, 256)
        for plane in range(2):
            fe[2 * j + plane + 1, 1:9, :, 0:256] = moved[plane]
    for px in range(-1, 8):
        for py in range(-1, 8):
            dx, dy = (-1 if px < 0 else 0), (-1 if py < 0 else 0)
            tile = fe[px % 8 + 1, py % 8 + 1, :, 0:256]
            if dx or dy:
                fe[px + 1, py + 1, :, 0:256] = sublane_gather(tile, pick[dx, dy, 0])
            fe[px + 1, py + 1, :, 256:384] = sublane_gather(tile[:, 128:256], pick[dx, dy, -1])
    for tap, (kx, ky) in enumerate(TAPS):
        rows = [fe[2 * x + kx, 2 * y + ky] for x in range(4) for y in range(4)]
        p1[:, tap * 384 : tap * 384 + 384] = jnp.concatenate(rows, axis=0).astype(BF16)


def half_patches(pick, value, ext, patches):
    low = iota((NB, 128), 1) < 64
    for px in range(-1, 5):
        for py in range(-1, 5):
            dx = -1 if px < 0 else (1 if px > 3 else 0)
            dy = -1 if py < 0 else (1 if py > 3 else 0)
            at = ((px % 4) * 4 + py % 4) * 8
            tile = value[at : at + 8]
            if dx or dy:
                ext[px + 1, py + 1, :, 0:256] = sublane_gather(tile, pick[dx, dy, 0])
            else:
                ext[px + 1, py + 1, :, 0:256] = tile
            above = sublane_gather(tile[:, 0:128], pick[dx, dy, 1])
            below = sublane_gather(tile[:, 128:256], pick[dx, dy, -1])
            ext[px + 1, py + 1, :, 256:384] = jnp.where(low, above, below)
    for tap, (kx, ky) in enumerate(TAPS):
        rows = [ext[x + kx, y + ky] for x in range(4) for y in range(4)]
        patches[:, tap * 384 : tap * 384 + 384] = jnp.concatenate(rows, axis=0).astype(BF16)


def halves(parts):
    size = parts[0].shape[0] // 2
    lo, hi = parts[0] + parts[2], parts[1] + parts[3]
    return [(lo[:size], hi[:size]), (lo[size:], hi[size:])]


def fold(pay, lower, upper, target):
    size = lower[0].shape[0]
    is_low = iota((size, 128), 1) < 64
    keep = jnp.where(is_low, lower[0], upper[1])
    turn = jnp.where(is_low, upper[0], lower[1])
    pay[target : target + size, :] = keep + pltpu.roll(turn, 64, 1)


def second_grad(p2, d_second, pay):
    blocks = []
    for tap in range(9):
        full = dot(p2[:, tap * 384 : tap * 384 + 384], d_second, ((0,), (0,)))
        blocks += halves([
            jnp.concatenate([full[320:384, 0:128], full[0:128, 0:128]], axis=0),
            full[0:192, 0:128],
            full[64:256, 128:256],
            full[128:320, 128:256],
        ])
    for at in range(9):
        fold(pay, blocks[at], blocks[at + 9], 432 + at * 96)


def first_grad(p1, d_pre, pay):
    blocks = []
    for tap in range(9):
        full = dot(p1[:, tap * 384 : tap * 384 + 384], d_pre, ((0,), (0,)))
        parts = [jnp.concatenate([full[352:384, 0:128], full[0:64, 0:128]], axis=0)]
        for zo in range(1, 4):
            at, lane = 32 * (2 * zo - 1), 128 * (zo // 2)
            parts.append(full[at : at + 96, lane : lane + 128])
        blocks += halves(parts)
    for at in range(9):
        fold(pay, blocks[at], blocks[at + 9], at * 48)


def scene_step(pick, upstream, bricks_ref, dec_ref, pay, fe, he, de, wide1, wide2, wide3, p1, p2, p3):
    first_patches(pick, bricks_ref, fe, p1)
    pre = dot(p1[...], wide1[...])
    sig_pre = jax.nn.sigmoid(pre)
    hidden = (pre * sig_pre).astype(BF16)
    half_patches(pick, hidden.astype(F32), he, p2)
    second = dot(p2[...], wide2[...])
    sig = jax.nn.sigmoid(second)
    dec_ref[...] = (second * sig).astype(BF16)
    d_second = (upstream * (sig * (1.0 + second * (1.0 - sig)))).astype(BF16)
    second_grad(p2, d_second, pay)
    half_patches(pick, d_second.astype(F32), de, p3)
    d_hidden = dot(p3[...], wide3[...]).astype(BF16)
    d_pre = (d_hidden.astype(F32) * (sig_pre * (1.0 + pre * (1.0 - sig_pre)))).astype(BF16)
    first_grad(p1, d_pre, pay)
    pay[1296:1536, :] = jnp.zeros((240, 128), F32)


def train_kernel(factor, assign_ref, owner_ref, occ_ref, feats_hbm, w1_hbm, w2_hbm, cot_hbm,
                 out_ref, dec_ref, own_ref,
                 feats, w1, w2, cot, packed, stage, bricks,
                 fe, he, de, wide1, wide2, wide3, p1, p2, p3, pay,
                 from_core, mine, from_scene, part, from_z,
                 load_sem, send_sem, recv_sem,
                 core_send, core_recv, scene_send, scene_recv, z_send, z_recv,
                 out_send, out_recv, back_send, back_recv):
    tile, scene = lax.axis_index("tile"), lax.axis_index("scene")
    core = lax.rem(tile, 2)
    z = tile // 2
    sibling = 2 * z + 1 - core
    loads = []
    for at in range(4):
        loads.append(pltpu.make_async_copy(
            feats_hbm.at[pl.ds(4 * at, 4)], feats.at[pl.ds(4 * at, 4)], load_sem.at[at]))
    for at, (src, dst) in enumerate(((w1_hbm, w1), (w2_hbm, w2), (cot_hbm, cot))):
        loads.append(pltpu.make_async_copy(src, dst, load_sem.at[4 + at]))
    for load in loads:
        load.start()
    barrier = pltpu.get_barrier_semaphore()
    for step in range(1, 16):
        pl.semaphore_signal(barrier, inc=1, device_id={"tile": lax.rem(tile + step, 16)}, device_id_type=MESH)
        pl.semaphore_signal(barrier, inc=1, device_id={"scene": lax.rem(scene + step, 16)}, device_id_type=MESH)

    slots = row_codes([occ_ref[tile // 4, by] for by in range(4)])
    for j in range(SCENES):
        if j % 4 == 0:
            loads[j // 4].wait()
        pack_scene(feats, j, slots, packed)
    bricks[tile] = packed[scene_of(assign_ref, tile)]
    pl.semaphore_wait(barrier, 30)
    sends = []
    for step in range(1, SCENES):
        peer = lax.rem(tile + step, SCENES)
        stage[peer] = packed[scene_of(assign_ref, peer)]
        copy = remote(stage.at[peer], bricks.at[tile], send_sem.at[step], recv_sem.at[step], {"tile": peer})
        copy.start()
        sends.append(copy)

    own = own_codes(occ_ref, owner_ref[...], tile)
    own_ref[...] = own
    loads[4].wait()
    loads[5].wait()
    banded(w1, w2, wide1, wide2, wide3)
    pick = pickers(own)
    loads[6].wait()
    upstream = upstream_bricks(own, cot)
    for copy in sends:
        copy.wait_recv()

    scene_step(pick, upstream, bricks, dec_ref, pay, fe, he, de, wide1, wide2, wide3, p1, p2, p3)

    def rows(half, owner):
        return pl.ds(pl.multiple_of((half * 16 + owner) * CHUNK, CHUNK), CHUNK)

    waits = list(sends)
    cores = []
    for step in range(16):
        owner = lax.rem(scene + step, 16)
        copy = remote(
            pay.at[rows(1 - core, owner)], from_core.at[owner], core_send.at[step], core_recv.at[step],
            {"tile": sibling},
        )
        copy.start()
        cores.append(copy)
    waits += cores
    scenes = []
    for step in list(range(1, 16)) + [0]:
        owner = lax.rem(scene + step, 16)
        cores[step].wait_recv()
        added = (pay[rows(core, owner)] + from_core[owner]).astype(BF16)
        if step == 0:
            from_scene[scene] = added
            continue
        mine[owner] = added
        copy = remote(
            mine.at[owner], from_scene.at[scene], scene_send.at[step], scene_recv.at[step], {"scene": owner}
        )
        copy.start()
        scenes.append(copy)
    waits += scenes
    for copy in scenes:
        copy.wait_recv()
    total = from_scene[0].astype(F32)
    for k in range(1, 16):
        total = total + from_scene[k].astype(F32)
    part[...] = total.astype(BF16)
    from_z[z] = total.astype(BF16)
    zs = []
    for step in range(1, 8):
        peer = lax.rem(z + step, 8)
        copy = remote(part, from_z.at[z], z_send.at[step], z_recv.at[step], {"tile": 2 * peer + core})
        copy.start()
        zs.append(copy)
    waits += zs
    for copy in zs:
        copy.wait_recv()
    total = from_z[0].astype(F32)
    for k in range(1, 8):
        total = total + from_z[k].astype(F32)
    out_ref[rows(core, scene)] = (total * factor).astype(BF16)
    outs = [None]
    backs = []
    for step in range(1, 16):
        here = out_ref.at[rows(core, scene)]
        copy = remote(here, here, out_send.at[step], out_recv.at[step], {"scene": lax.rem(scene + step, 16)})
        copy.start()
        outs.append(copy)
    waits += outs[1:]
    for step in range(16):
        if step:
            outs[step].wait_recv()
        here = out_ref.at[rows(core, lax.rem(scene - step + 16, 16))]
        copy = remote(here, here, back_send.at[step], back_recv.at[step], {"tile": sibling})
        copy.start()
        backs.append(copy)
    waits += backs
    for copy in backs:
        copy.wait_recv()
    for copy in waits:
        copy.wait_send()


def compute_scratch():
    wide = pltpu.VMEM((3456, 256), BF16)
    patch = pltpu.VMEM((128, 3456), BF16)
    return [
        pltpu.VMEM((9, 9, 8, 384), F32),
        pltpu.VMEM((6, 6, 8, 384), F32),
        pltpu.VMEM((6, 6, 8, 384), F32),
        wide, wide, wide, patch, patch, patch,
    ]


def train(assign, occupancy, feats, w1, w2, cot, factor):
    sem = lambda n: pltpu.SemaphoreType.DMA((n,))
    chunk = lambda n, dtype: pltpu.VMEM((n, CHUNK, 128), dtype)
    anyspace = pl.BlockSpec(memory_space=pl.ANY)
    return pl.pallas_call(
        functools.partial(train_kernel, factor),
        out_shape=[
            jax.ShapeDtypeStruct((32 * CHUNK, 128), BF16),
            jax.ShapeDtypeStruct((128, 256), BF16),
            jax.ShapeDtypeStruct((NB, 128), I32),
        ],
        in_specs=[smem(), vmem(), vmem()] + [anyspace] * 4,
        out_specs=[vmem()] * 3,
        scratch_shapes=[
            pltpu.VMEM(feats.shape, BF16),
            pltpu.VMEM(w1.shape, BF16),
            pltpu.VMEM(w2.shape, BF16),
            pltpu.VMEM(cot.shape, BF16),
            pltpu.VMEM((SCENES, 32, 256), BF16),
            pltpu.VMEM((SCENES, 32, 256), BF16),
            pltpu.VMEM((SCENES, 32, 256), BF16),
            *compute_scratch(),
            pltpu.VMEM((32 * CHUNK, 128), F32),
            chunk(16, F32), chunk(16, BF16), chunk(16, BF16),
            pltpu.VMEM((CHUNK, 128), BF16),
            chunk(8, BF16),
            sem(7), sem(16), sem(16),
            sem(16), sem(16), sem(16), sem(16), sem(8), sem(8), sem(16), sem(16), sem(16), sem(16),
        ],
        compiler_params=pltpu.CompilerParams(collective_id=0, has_side_effects=True, vmem_limit_bytes=VMEM_LIMIT),
        name="train",
    )(assign, assign, occupancy.transpose(1, 2, 3, 0), feats, w1, w2, cot)


def unpack_kernel(code_ref, total_ref, compact_ref, first_ref, second_ref, dec_ref):
    row, col = iota((64, 128), 0), iota((64, 128), 1)
    for half in range(2):
        pick = jnp.where(col == row + 64 * half, 1.0, 0.0).astype(BF16)
        first_ref[:, 432 * half : 432 * half + 432] = dot(pick, total_ref[0:432], ((1,), (1,)))
        second_ref[:, 864 * half : 864 * half + 864] = dot(pick, total_ref[432:1296], ((1,), (1,)))
    codes = [code_ref[b, 0] for b in range(NB)]
    bys = [code // 4 for code in codes]
    bzs = [code - 4 * by for code, by in zip(codes, bys)]
    row, col = iota((128, 32), 0), iota((128, 32), 1)
    goal = jnp.full((128, 32), -1, I32)
    for b in range(NB):
        start = jnp.where(codes[b] < NONE, 16 * b + 4 * bys[b], -10000)
        goal = jnp.where(col % 8 == b, start + col // 8, goal)
    give = jnp.where(row == goal, 1.0, 0.0).astype(BF16)
    for x in range(4):
        spread = dot(give, compact_ref[32 * x : 32 * x + 32])
        for bx in range(BX):
            one, two = spread[32 * bx : 32 * bx + 16], spread[32 * bx + 16 : 32 * bx + 32]
            for c in range(4):
                block = jnp.where(bzs[2 * bx] == c, one, 0.0) + jnp.where(bzs[2 * bx + 1] == c, two, 0.0)
                dec_ref[4 * bx + x, :, 256 * c : 256 * c + 256] = block.astype(BF16)


def unpack(code, total, compact):
    return pl.pallas_call(
        unpack_kernel,
        out_shape=[
            jax.ShapeDtypeStruct((64, 864), F32),
            jax.ShapeDtypeStruct((64, 1728), F32),
            jax.ShapeDtypeStruct((16, 16, 1024), BF16),
        ],
        in_specs=[smem(), vmem(), vmem()],
        out_specs=[vmem()] * 3,
        compiler_params=pltpu.CompilerParams(vmem_limit_bytes=VMEM_LIMIT),
        name="unpack",
    )(code, total, compact)


def per_device(feats, occupancy, assign, w_first, w_second, grad_out):
    factor = 1.0 / math.sqrt(256 * 16 * 16 * 16)
    total, compact, code = train(assign, occupancy, feats, w_first.T, w_second.T, grad_out[0], factor)
    grad_first, grad_second, decoded = unpack(code, total, compact)
    return decoded[None], grad_first.T, grad_second.T


def solution(mesh):
    return jax.shard_map(
        per_device,
        mesh=mesh,
        in_specs=(
            P("scene", "tile", None, None),
            P("scene", None, None, None),
            P("scene", None),
            P(),
            P(),
            P(("scene", "tile"), None, None, None),
        ),
        out_specs=(P(("scene", "tile"), None, None, None), P(), P()),
        check_vma=False,
    )
```

```python
import functools
import math

import jax
import jax.numpy as jnp
from jax import lax
from jax.experimental import pallas as pl
from jax.experimental.pallas import tpu as pltpu
from jax.sharding import PartitionSpec as P

MESH = pl.DeviceIdType.MESH
F32, BF16, I32 = jnp.float32, jnp.bfloat16, jnp.int32
SCENES, BX, SLOTS, NB = 16, 4, 2, 8
NONE = 16
TAPS = [(kx, ky) for kx in range(3) for ky in range(3)]
SECOND_ROWS, FIRST_ROWS = 32, 16
VMEM_LIMIT = 40 * 1024 * 1024


def vmem():
    return pl.BlockSpec(memory_space=pltpu.VMEM)


def smem():
    return pl.BlockSpec(memory_space=pltpu.SMEM)


def iota(shape, dim):
    return lax.broadcasted_iota(I32, shape, dim)


def dot(lhs, rhs, dims=((1,), (0,))):
    return lax.dot_general(lhs, rhs, (dims, ((), ())), preferred_element_type=F32)


def remote(src, dst, send, recv, device):
    return pltpu.make_async_remote_copy(
        src_ref=src, dst_ref=dst, send_sem=send, recv_sem=recv, device_id=device, device_id_type=MESH
    )


def row_codes(planes):
    first, last = NONE, -1
    for by in range(4):
        flags = planes[by] > 0
        ids = iota(planes[by].shape, 0) + 4 * by
        first = jnp.minimum(first, jnp.where(flags, ids, NONE))
        last = jnp.maximum(last, jnp.where(flags, ids, -1))
    first = jnp.min(first.astype(F32), axis=0, keepdims=True).astype(I32)
    last = jnp.max(last.astype(F32), axis=0, keepdims=True).astype(I32)
    return first, jnp.where(last > first, last, NONE)


def pack_scene(feats_ref, scene, slots, packed):
    marks = [jnp.broadcast_to(code[:, scene : scene + 1], (8, 256)) for code in slots]
    bys = [mark // 4 for mark in marks]
    bzs = [mark % 4 for mark in marks]
    rows = [[None, None], [None, None]]
    for plane in range(2):
        wide = feats_ref[scene, plane].astype(F32)
        for slot in range(SLOTS):
            acc = jnp.zeros((8, 256), F32)
            for by in range(4):
                line = wide[8 * by : 8 * by + 8]
                part = line[:, 0:256]
                for bz in range(1, 4):
                    part = jnp.where(bzs[slot] == bz, line[:, 256 * bz : 256 * bz + 256], part)
                acc = jnp.where(bys[slot] == by, part, acc)
            rows[slot][plane] = acc
    packed[scene] = jnp.concatenate(rows[0] + rows[1], axis=0).astype(BF16)


def scene_of(assign_ref, target):
    scene = 0
    for j in range(SCENES):
        scene = jnp.where(assign_ref[0, j] == target, j, scene)
    return scene


def own_codes(occ_ref, owner, me):
    codes = []
    for bx in range(BX):
        codes += row_codes([occ_ref[bx, by] for by in range(4)])
    mine = jnp.where(owner == me, jnp.concatenate(codes, axis=0), 0)
    own = jnp.sum(mine.astype(F32), axis=1, keepdims=True).astype(I32)
    return jnp.broadcast_to(own, (NB, 128))


def sublane_gather(value, picker):
    index, hit = picker
    pieces = []
    for at in range(0, value.shape[1], 128):
        got = jnp.take_along_axis(value[:, at : at + 128], index, axis=0)
        pieces.append(jnp.where(hit, got, 0.0))
    return pieces[0] if len(pieces) == 1 else jnp.concatenate(pieces, axis=1)


def pickers(own):
    sub = iota((NB, 128), 0)
    place = jnp.where(own < NONE, (sub // 2) * 64 + (own // 4) * 8 + own % 4, -10000 * (sub + 1))
    each = [jnp.broadcast_to(place[b : b + 1], (NB, 128)) for b in range(NB)]
    pick = {}
    for dx in (-1, 0, 1):
        for dy in (-1, 0, 1):
            for dz in (-1, 0, 1):
                if (dx, dy, dz) == (0, 0, 0):
                    continue
                target = place + (dx * 64 + dy * 8 + dz)
                index = jnp.zeros((NB, 128), I32)
                hit = jnp.zeros((NB, 128), I32)
                for b in range(NB):
                    same = target == each[b]
                    index = jnp.where(same, b, index)
                    hit = jnp.where(same, 1, hit)
                pick[dx, dy, dz] = index, hit > 0
    return pick


def banded(w1_ref, w2_ref, wide1, wide2, wide3):
    wide1[...] = jnp.zeros_like(wide1)
    wide2[...] = jnp.zeros_like(wide2)
    wide3[...] = jnp.zeros_like(wide3)

    def turned(ref):
        return ref[...].astype(F32).T.astype(BF16)

    first, second = turned(w1_ref), turned(w2_ref)
    for tap in range(9):
        base = tap * 384
        w = first[tap * 96 : tap * 96 + 96]
        wide1[base + 352 : base + 384, 0:64] = w[0:32]
        wide1[base : base + 64, 0:64] = w[32:96]
        for zo in range(1, 4):
            at = base + 32 * (2 * zo - 1)
            wide1[at : at + 96, 64 * zo : 64 * zo + 64] = w
        forward = [second[(3 * tap + kz) * 64 : (3 * tap + kz) * 64 + 64] for kz in range(3)]
        backward = [w2_ref[:, (26 - 3 * tap - kz) * 64 : (26 - 3 * tap - kz) * 64 + 64] for kz in range(3)]
        for target, blocks in ((wide2, forward), (wide3, backward)):
            for zo in range(4):
                for kz in range(3):
                    zi = zo + kz - 1
                    at = base + (320 if zi < 0 else 64 * zi)
                    target[at : at + 64, 64 * zo : 64 * zo + 64] = blocks[kz]


def upstream_bricks(own, cot_ref):
    row, col = iota((32, 128), 0), iota((32, 128), 1)
    start = jnp.where(own < NONE, iota((NB, 128), 0) * 16 + (own // 4) * 4, -10000)
    goal = jnp.concatenate([start] * 4, axis=0) + row // 8
    take = jnp.where(col == goal, 1.0, 0.0).astype(BF16)
    bzs = own % 4
    marks = [jnp.broadcast_to(bzs[b : b + 1, 0:1], (16, 256)) for b in range(NB)]
    ups = []
    for x in range(4):
        planes = []
        for bx in range(BX):
            wide = cot_ref[4 * bx + x].astype(F32)
            for slot in range(SLOTS):
                part = wide[:, 0:256]
                for bz in range(1, 4):
                    part = jnp.where(marks[2 * bx + slot] == bz, wide[:, 256 * bz : 256 * bz + 256], part)
                planes.append(part)
        ups.append(dot(take, jnp.concatenate(planes, axis=0).astype(BF16)))
    return jnp.concatenate(ups, axis=0)


def first_patches(pick, bricks_ref, fe, p1):
    row, col = iota((128, 128), 0), iota((128, 128), 1)
    source = ((row // 2) % 4) * 32 + (row % 2) * 16 + (row // 64) * 8 + (row // 8) % 8
    perm = jnp.where(col == source, 1.0, 0.0).astype(BF16)
    for j in range(4):
        stack = jnp.concatenate([bricks_ref[4 * bx + j] for bx in range(BX)], axis=0)
        moved = dot(perm, stack).reshape(2, 8, 8, 256)
        for plane in range(2):
            fe[2 * j + plane + 1, 1:9, :, 0:256] = moved[plane]
    for px in range(-1, 8):
        for py in range(-1, 8):
            dx, dy = (-1 if px < 0 else 0), (-1 if py < 0 else 0)
            tile = fe[px % 8 + 1, py % 8 + 1, :, 0:256]
            if dx or dy:
                fe[px + 1, py + 1, :, 0:256] = sublane_gather(tile, pick[dx, dy, 0])
            fe[px + 1, py + 1, :, 256:384] = sublane_gather(tile[:, 128:256], pick[dx, dy, -1])
    for tap, (kx, ky) in enumerate(TAPS):
        rows = [fe[2 * x + kx, 2 * y + ky] for x in range(4) for y in range(4)]
        p1[:, tap * 384 : tap * 384 + 384] = jnp.concatenate(rows, axis=0).astype(BF16)


def half_patches(pick, value, ext, patches):
    low = iota((NB, 128), 1) < 64
    for px in range(-1, 5):
        for py in range(-1, 5):
            dx = -1 if px < 0 else (1 if px > 3 else 0)
            dy = -1 if py < 0 else (1 if py > 3 else 0)
            at = ((px % 4) * 4 + py % 4) * 8
            tile = value[at : at + 8]
            if dx or dy:
                ext[px + 1, py + 1, :, 0:256] = sublane_gather(tile, pick[dx, dy, 0])
            else:
                ext[px + 1, py + 1, :, 0:256] = tile
            above = sublane_gather(tile[:, 0:128], pick[dx, dy, 1])
            below = sublane_gather(tile[:, 128:256], pick[dx, dy, -1])
            ext[px + 1, py + 1, :, 256:384] = jnp.where(low, above, below)
    for tap, (kx, ky) in enumerate(TAPS):
        rows = [ext[x + kx, y + ky] for x in range(4) for y in range(4)]
        patches[:, tap * 384 : tap * 384 + 384] = jnp.concatenate(rows, axis=0).astype(BF16)


def halves(parts):
    size = parts[0].shape[0] // 2
    lo, hi = parts[0] + parts[2], parts[1] + parts[3]
    return [(lo[:size], hi[:size]), (lo[size:], hi[size:])]


def fold(pay, lower, upper, target):
    size = lower[0].shape[0]
    is_low = iota((size, 128), 1) < 64
    keep = jnp.where(is_low, lower[0], upper[1])
    turn = jnp.where(is_low, upper[0], lower[1])
    pay[target : target + size, :] = keep + pltpu.roll(turn, 64, 1)


def second_grad(p2, d_second, pay):
    blocks = []
    for tap in range(9):
        full = dot(p2[:, tap * 384 : tap * 384 + 384], d_second, ((0,), (0,)))
        blocks += halves([
            jnp.concatenate([full[320:384, 0:128], full[0:128, 0:128]], axis=0),
            full[0:192, 0:128],
            full[64:256, 128:256],
            full[128:320, 128:256],
        ])
    for at in range(9):
        fold(pay, blocks[at], blocks[at + 9], at * 96)


def first_grad(p1, d_pre, pay):
    blocks = []
    for tap in range(9):
        full = dot(p1[:, tap * 384 : tap * 384 + 384], d_pre, ((0,), (0,)))
        parts = [jnp.concatenate([full[352:384, 0:128], full[0:64, 0:128]], axis=0)]
        for zo in range(1, 4):
            at, lane = 32 * (2 * zo - 1), 128 * (zo // 2)
            parts.append(full[at : at + 96, lane : lane + 128])
        blocks += halves(parts)
    for at in range(9):
        fold(pay, blocks[at], blocks[at + 9], at * 48)


def forward(pick, upstream, bricks_ref, dec_ref, pay2, fe, he, wide1, wide2, p1, p2):
    first_patches(pick, bricks_ref, fe, p1)
    pre = dot(p1[...], wide1[...])
    sig_pre = jax.nn.sigmoid(pre)
    hidden = (pre * sig_pre).astype(BF16)
    half_patches(pick, hidden.astype(F32), he, p2)
    second = dot(p2[...], wide2[...])
    sig = jax.nn.sigmoid(second)
    dec_ref[...] = (second * sig).astype(BF16)
    d_second = (upstream * (sig * (1.0 + second * (1.0 - sig)))).astype(BF16)
    second_grad(p2, d_second, pay2)
    return sig_pre * (1.0 + pre * (1.0 - sig_pre)), d_second


def hidden_grad(pick, slope, d_second, de, wide3, p3):
    half_patches(pick, d_second.astype(F32), de, p3)
    d_hidden = dot(p3[...], wide3[...]).astype(BF16)
    return (d_hidden.astype(F32) * slope).astype(BF16)


class Total:
    def __init__(self, rows, factor, pay, out, from_core, mine, from_scene, part, from_z, send, recv):
        self.rows, self.factor = rows, factor
        self.pay, self.out, self.from_core, self.mine = pay, out, from_core, mine
        self.from_scene, self.part, self.from_z, self.send, self.recv = from_scene, part, from_z, send, recv
        tile = lax.axis_index("tile")
        self.scene, self.core, self.z = lax.axis_index("scene"), lax.rem(tile, 2), tile // 2
        self.sibling = {"tile": 2 * self.z + 1 - self.core}
        self.started = []

    def chunk(self, half, owner):
        return pl.ds(pl.multiple_of((half * 16 + owner) * self.rows, self.rows), self.rows)

    def copy(self, src, dst, kind, step, device):
        copy = remote(src, dst, self.send.at[kind, step], self.recv.at[kind, step], device)
        copy.start()
        self.started.append(copy)
        return copy

    def owner(self, step):
        return lax.rem(self.scene + step, 16)

    def to_core(self):
        self.cores = []
        for step in range(16):
            owner = self.owner(step)
            self.cores.append(self.copy(
                self.pay.at[self.chunk(1 - self.core, owner)], self.from_core.at[owner], 0, step, self.sibling))

    def to_scene(self):
        self.scenes = []
        for step in list(range(1, 16)) + [0]:
            owner = self.owner(step)
            self.cores[step].wait_recv()
            added = (self.pay[self.chunk(self.core, owner)] + self.from_core[owner]).astype(BF16)
            if step == 0:
                self.from_scene[self.scene] = added
                continue
            self.mine[owner] = added
            self.scenes.append(self.copy(
                self.mine.at[owner], self.from_scene.at[self.scene], 1, step, {"scene": owner}))

    def to_z(self):
        for copy in self.scenes:
            copy.wait_recv()
        total = self.from_scene[0].astype(F32)
        for k in range(1, 16):
            total = total + self.from_scene[k].astype(F32)
        self.part[...] = total.astype(BF16)
        self.from_z[self.z] = total.astype(BF16)
        self.zs = []
        for step in range(1, 8):
            peer = lax.rem(self.z + step, 8)
            self.zs.append(self.copy(
                self.part, self.from_z.at[self.z], 2, step, {"tile": 2 * peer + self.core}))

    def to_all(self):
        for copy in self.zs:
            copy.wait_recv()
        total = self.from_z[0].astype(F32)
        for k in range(1, 8):
            total = total + self.from_z[k].astype(F32)
        here = self.out.at[self.chunk(self.core, self.scene)]
        here[...] = (total * self.factor).astype(BF16)
        self.outs = [None]
        for step in range(1, 16):
            self.outs.append(self.copy(here, here, 3, step, {"scene": self.owner(step)}))

    def back(self):
        self.backs = []
        for step in range(16):
            if step:
                self.outs[step].wait_recv()
            here = self.out.at[self.chunk(self.core, lax.rem(self.scene - step + 16, 16))]
            self.backs.append(self.copy(here, here, 4, step, self.sibling))

    def finish(self):
        for copy in self.backs:
            copy.wait_recv()
        for copy in self.started:
            copy.wait_send()


def total_scratch(rows):
    chunk = lambda n, dtype: pltpu.VMEM((n, rows, 128), dtype)
    return [
        pltpu.VMEM((32 * rows, 128), F32),
        chunk(16, F32), chunk(16, BF16), chunk(16, BF16),
        pltpu.VMEM((rows, 128), BF16),
        chunk(8, BF16),
        pltpu.SemaphoreType.DMA((5, 16)),
        pltpu.SemaphoreType.DMA((5, 16)),
    ]


def train_kernel(factor, assign_hbm, occ_hbm, feats_hbm, w1_hbm, w2_hbm, cot_hbm,
                 out1_ref, out2_ref, dec_ref, own_ref,
                 assign_ref, owner_ref, occ_ref, feats, w1, w2, cot, packed, stage, bricks,
                 fe, he, de, wide1, wide2, wide3, p1, p2, p3,
                 load_sem, send_sem, recv_sem, *totals):
    tile, scene = lax.axis_index("tile"), lax.axis_index("scene")
    barrier = pltpu.get_barrier_semaphore()
    for step in (8, 7, 9, 6, 10, 5, 11, 4, 12, 3, 13, 2, 14, 1, 15):
        pl.semaphore_signal(barrier, inc=1, device_id={"tile": lax.rem(tile + step, 16)}, device_id_type=MESH)
        pl.semaphore_signal(barrier, inc=1, device_id={"scene": lax.rem(scene + step, 16)}, device_id_type=MESH)
    pieces = [(assign_hbm, assign_ref), (assign_hbm, owner_ref), (occ_hbm, occ_ref)]
    pieces += [(feats_hbm.at[pl.ds(4 * at, 4)], feats.at[pl.ds(4 * at, 4)]) for at in range(4)]
    pieces += [(w1_hbm, w1), (w2_hbm, w2), (cot_hbm, cot)]
    loads = [pltpu.make_async_copy(src, dst, load_sem.at[at]) for at, (src, dst) in enumerate(pieces)]
    for load in loads:
        load.start()
    pay1, pay2 = totals[0], totals[8]
    sum1 = Total(FIRST_ROWS, factor, pay1, out1_ref, *totals[1:8])
    sum2 = Total(SECOND_ROWS, factor, pay2, out2_ref, *totals[9:16])

    for load in loads[:3]:
        load.wait()
    slots = row_codes([occ_ref[tile // 4, by] for by in range(4)])
    for j in range(SCENES):
        if j % 4 == 0:
            loads[3 + j // 4].wait()
        pack_scene(feats, j, slots, packed)
    bricks[tile] = packed[scene_of(assign_ref, tile)]
    pl.semaphore_wait(barrier, 30)
    sends = []
    for step in range(1, SCENES):
        peer = lax.rem(tile + step, SCENES)
        stage[peer] = packed[scene_of(assign_ref, peer)]
        copy = remote(stage.at[peer], bricks.at[tile], send_sem.at[step], recv_sem.at[step], {"tile": peer})
        copy.start()
        sends.append(copy)

    own = own_codes(occ_ref, owner_ref[...], tile)
    own_ref[...] = own
    loads[7].wait()
    loads[8].wait()
    banded(w1, w2, wide1, wide2, wide3)
    pick = pickers(own)
    loads[9].wait()
    upstream = upstream_bricks(own, cot)
    pay1[432:512, :] = jnp.zeros((80, 128), F32)
    pay2[864:1024, :] = jnp.zeros((160, 128), F32)
    for copy in sends:
        copy.wait_recv()

    slope, d_second = forward(pick, upstream, bricks, dec_ref, pay2, fe, he, wide1, wide2, p1, p2)
    sum2.to_core()
    d_pre = hidden_grad(pick, slope, d_second, de, wide3, p3)
    sum2.to_scene()
    first_grad(p1, d_pre, pay1)
    sum1.to_core()
    sum1.to_scene()
    sum2.to_z()
    sum1.to_z()
    sum2.to_all()
    sum1.to_all()
    sum2.back()
    sum1.back()
    sum2.finish()
    sum1.finish()
    for copy in sends:
        copy.wait_send()


def compute_scratch():
    wide = pltpu.VMEM((3456, 256), BF16)
    patch = pltpu.VMEM((128, 3456), BF16)
    return [
        pltpu.VMEM((9, 9, 8, 384), F32),
        pltpu.VMEM((6, 6, 8, 384), F32),
        pltpu.VMEM((6, 6, 8, 384), F32),
        wide, wide, wide, patch, patch, patch,
    ]


def train(assign, occupancy, feats, w1, w2, cot, factor):
    sem = lambda n: pltpu.SemaphoreType.DMA((n,))
    anyspace = pl.BlockSpec(memory_space=pltpu.HBM)
    planes = occupancy.transpose(1, 2, 3, 0)
    return pl.pallas_call(
        functools.partial(train_kernel, factor),
        out_shape=[
            pltpu.VMEM((32 * FIRST_ROWS, 128), BF16),
            pltpu.VMEM((32 * SECOND_ROWS, 128), BF16),
            pltpu.VMEM((128, 256), BF16),
            pltpu.VMEM((NB, 128), I32),
        ],
        in_specs=[anyspace] * 6,
        out_specs=[vmem()] * 4,
        scratch_shapes=[
            pltpu.SMEM(assign.shape, I32),
            pltpu.VMEM(assign.shape, I32),
            pltpu.VMEM(planes.shape, I32),
            pltpu.VMEM(feats.shape, BF16),
            pltpu.VMEM(w1.shape, BF16),
            pltpu.VMEM(w2.shape, BF16),
            pltpu.VMEM(cot.shape, BF16),
            pltpu.VMEM((SCENES, 32, 256), BF16),
            pltpu.VMEM((SCENES, 32, 256), BF16),
            pltpu.VMEM((SCENES, 32, 256), BF16),
            *compute_scratch(),
            sem(10), sem(16), sem(16),
            *total_scratch(FIRST_ROWS),
            *total_scratch(SECOND_ROWS),
        ],
        compiler_params=pltpu.CompilerParams(collective_id=0, has_side_effects=True, vmem_limit_bytes=VMEM_LIMIT),
        name="train",
    )(*(pltpu.with_memory_space_constraint(x, pltpu.HBM) for x in (assign, planes, feats, w1, w2, cot)))


def unpack_kernel(code_ref, total1_ref, total2_ref, compact_ref, first_hbm, second_hbm, dec_hbm,
                  first_ref, second_ref, dec_ref, sem):
    codes = [code_ref[b, 0] for b in range(NB)]
    bys = [code // 4 for code in codes]
    bzs = [code - 4 * by for code, by in zip(codes, bys)]
    row, col = iota((128, 32), 0), iota((128, 32), 1)
    goal = jnp.full((128, 32), -1, I32)
    for b in range(NB):
        start = jnp.where(codes[b] < NONE, 16 * b + 4 * bys[b], -10000)
        goal = jnp.where(col % 8 == b, start + col // 8, goal)
    give = jnp.where(row == goal, 1.0, 0.0).astype(BF16)
    for x in range(4):
        spread = dot(give, compact_ref[32 * x : 32 * x + 32])
        for bx in range(BX):
            one, two = spread[32 * bx : 32 * bx + 16], spread[32 * bx + 16 : 32 * bx + 32]
            for c in range(4):
                block = jnp.where(bzs[2 * bx] == c, one, 0.0) + jnp.where(bzs[2 * bx + 1] == c, two, 0.0)
                dec_ref[4 * bx + x, :, 256 * c : 256 * c + 256] = block.astype(BF16)
    stores = [pltpu.make_async_copy(dec_ref, dec_hbm, sem.at[0])]
    stores[0].start()
    row, col = iota((64, 128), 0), iota((64, 128), 1)
    picks = [jnp.where(col == row + 64 * half, 1.0, 0.0).astype(BF16) for half in range(2)]
    jobs = ((second_ref, second_hbm, total2_ref, 864), (first_ref, first_hbm, total1_ref, 432))
    for at, (ref, hbm, total_ref, count) in enumerate(jobs):
        for half in range(2):
            ref[:, count * half : count * half + count] = dot(picks[half], total_ref[0:count], ((1,), (1,)))
        stores.append(pltpu.make_async_copy(ref, hbm, sem.at[1 + at]))
        stores[-1].start()
    for store in stores:
        store.wait()


def unpack(code, total1, total2, compact):
    return pl.pallas_call(
        unpack_kernel,
        out_shape=[
            jax.ShapeDtypeStruct((64, 864), F32),
            jax.ShapeDtypeStruct((64, 1728), F32),
            jax.ShapeDtypeStruct((16, 16, 1024), BF16),
        ],
        in_specs=[smem(), vmem(), vmem(), vmem()],
        out_specs=[pl.BlockSpec(memory_space=pl.ANY)] * 3,
        scratch_shapes=[
            pltpu.VMEM((64, 864), F32),
            pltpu.VMEM((64, 1728), F32),
            pltpu.VMEM((16, 16, 1024), BF16),
            pltpu.SemaphoreType.DMA((3,)),
        ],
        compiler_params=pltpu.CompilerParams(vmem_limit_bytes=VMEM_LIMIT),
        name="unpack",
    )(code, total1, total2, compact)


def per_device(feats, occupancy, assign, w_first, w_second, grad_out):
    factor = 1.0 / math.sqrt(256 * 16 * 16 * 16)
    total1, total2, compact, code = train(assign, occupancy, feats, w_first.T, w_second.T, grad_out[0], factor)
    grad_first, grad_second, decoded = unpack(code, total1, total2, compact)
    return decoded[None], grad_first.T, grad_second.T


def solution(mesh):
    return jax.shard_map(
        per_device,
        mesh=mesh,
        in_specs=(
            P("scene", "tile", None, None),
            P("scene", None, None, None),
            P("scene", None),
            P(),
            P(),
            P(("scene", "tile"), None, None, None),
        ),
        out_specs=(P(("scene", "tile"), None, None, None), P(), P()),
        check_vma=False,
    )
```

```python
import functools
import math

import jax
import jax.numpy as jnp
from jax import lax
from jax.experimental import pallas as pl
from jax.experimental.pallas import tpu as pltpu
from jax.sharding import PartitionSpec as P

MESH = pl.DeviceIdType.MESH
F32, BF16, I32 = jnp.float32, jnp.bfloat16, jnp.int32
SCENES, BX, SLOTS, NB = 16, 4, 2, 8
NONE = 16
TAPS = [(kx, ky) for kx in range(3) for ky in range(3)]
SECOND_ROWS, FIRST_ROWS = 32, 16
VMEM_LIMIT = 40 * 1024 * 1024
FAR_FIRST = (8, 7, 9, 6, 10, 5, 11, 4, 12, 3, 13, 2, 14, 1, 15)


def vmem():
    return pl.BlockSpec(memory_space=pltpu.VMEM)


def smem():
    return pl.BlockSpec(memory_space=pltpu.SMEM)


def iota(shape, dim):
    return lax.broadcasted_iota(I32, shape, dim)


def dot(lhs, rhs, dims=((1,), (0,))):
    return lax.dot_general(lhs, rhs, (dims, ((), ())), preferred_element_type=F32)


def remote(src, dst, send, recv, device):
    return pltpu.make_async_remote_copy(
        src_ref=src, dst_ref=dst, send_sem=send, recv_sem=recv, device_id=device, device_id_type=MESH
    )


def wait_bytes(ref, sem):
    pltpu.make_async_copy(ref, ref, sem).wait()


def row_codes(planes):
    first, last = NONE, -1
    for by in range(4):
        flags = planes[by] > 0
        ids = iota(planes[by].shape, 0) + 4 * by
        first = jnp.minimum(first, jnp.where(flags, ids, NONE))
        last = jnp.maximum(last, jnp.where(flags, ids, -1))
    first = jnp.min(first.astype(F32), axis=0, keepdims=True).astype(I32)
    last = jnp.max(last.astype(F32), axis=0, keepdims=True).astype(I32)
    return first, jnp.where(last > first, last, NONE)


def pack_scene(feats_ref, scene, slots, packed):
    marks = [jnp.broadcast_to(code[:, scene : scene + 1], (8, 256)) for code in slots]
    bys = [mark // 4 for mark in marks]
    bzs = [mark % 4 for mark in marks]
    rows = [[None, None], [None, None]]
    for plane in range(2):
        wide = feats_ref[scene, plane].astype(F32)
        for slot in range(SLOTS):
            acc = jnp.zeros((8, 256), F32)
            for by in range(4):
                line = wide[8 * by : 8 * by + 8]
                part = line[:, 0:256]
                for bz in range(1, 4):
                    part = jnp.where(bzs[slot] == bz, line[:, 256 * bz : 256 * bz + 256], part)
                acc = jnp.where(bys[slot] == by, part, acc)
            rows[slot][plane] = acc
    packed[scene] = jnp.concatenate(rows[0] + rows[1], axis=0).astype(BF16)


def scene_of(assign_ref, target):
    scene = 0
    for j in range(SCENES):
        scene = jnp.where(assign_ref[0, j] == target, j, scene)
    return scene


def own_codes(occ_ref, owner, me):
    codes = []
    for bx in range(BX):
        codes += row_codes([occ_ref[bx, by] for by in range(4)])
    mine = jnp.where(owner == me, jnp.concatenate(codes, axis=0), 0)
    own = jnp.sum(mine.astype(F32), axis=1, keepdims=True).astype(I32)
    return jnp.broadcast_to(own, (NB, 128))


def sublane_gather(value, picker):
    index, hit = picker
    pieces = []
    for at in range(0, value.shape[1], 128):
        got = jnp.take_along_axis(value[:, at : at + 128], index, axis=0)
        pieces.append(jnp.where(hit, got, 0.0))
    return pieces[0] if len(pieces) == 1 else jnp.concatenate(pieces, axis=1)


def pickers(own):
    sub = iota((NB, 128), 0)
    place = jnp.where(own < NONE, (sub // 2) * 64 + (own // 4) * 8 + own % 4, -10000 * (sub + 1))
    each = [jnp.broadcast_to(place[b : b + 1], (NB, 128)) for b in range(NB)]
    pick = {}
    for dx in (-1, 0, 1):
        for dy in (-1, 0, 1):
            for dz in (-1, 0, 1):
                if (dx, dy, dz) == (0, 0, 0):
                    continue
                target = place + (dx * 64 + dy * 8 + dz)
                index = jnp.zeros((NB, 128), I32)
                hit = jnp.zeros((NB, 128), I32)
                for b in range(NB):
                    same = target == each[b]
                    index = jnp.where(same, b, index)
                    hit = jnp.where(same, 1, hit)
                pick[dx, dy, dz] = index, hit > 0
    return pick


def banded(w1_ref, w2_ref, wide1, wide2, wide3):
    wide1[...] = jnp.zeros_like(wide1)
    wide2[...] = jnp.zeros_like(wide2)
    wide3[...] = jnp.zeros_like(wide3)

    def turned(ref):
        return ref[...].astype(F32).T.astype(BF16)

    first, second = turned(w1_ref), turned(w2_ref)
    for tap in range(9):
        base = tap * 384
        w = first[tap * 96 : tap * 96 + 96]
        wide1[base + 352 : base + 384, 0:64] = w[0:32]
        wide1[base : base + 64, 0:64] = w[32:96]
        for zo in range(1, 4):
            at = base + 32 * (2 * zo - 1)
            wide1[at : at + 96, 64 * zo : 64 * zo + 64] = w
        forward = [second[(3 * tap + kz) * 64 : (3 * tap + kz) * 64 + 64] for kz in range(3)]
        backward = [w2_ref[:, (26 - 3 * tap - kz) * 64 : (26 - 3 * tap - kz) * 64 + 64] for kz in range(3)]
        for target, blocks in ((wide2, forward), (wide3, backward)):
            for zo in range(4):
                for kz in range(3):
                    zi = zo + kz - 1
                    at = base + (320 if zi < 0 else 64 * zi)
                    target[at : at + 64, 64 * zo : 64 * zo + 64] = blocks[kz]


def takers(own):
    row, col = iota((32, 128), 0), iota((32, 128), 1)
    start = jnp.where(own < NONE, iota((NB, 128), 0) * 16 + (own // 4) * 4, -10000)
    goal = jnp.concatenate([start] * 4, axis=0) + row // 8
    take = jnp.where(col == goal, 1.0, 0.0).astype(BF16)
    bzs = own % 4
    return take, [jnp.broadcast_to(bzs[b : b + 1, 0:1], (16, 256)) for b in range(NB)]


def upstream_bricks(take, marks, cot_ref):
    ups = []
    for x in range(4):
        planes = []
        for bx in range(BX):
            wide = cot_ref[4 * bx + x].astype(F32)
            for slot in range(SLOTS):
                part = wide[:, 0:256]
                for bz in range(1, 4):
                    part = jnp.where(marks[2 * bx + slot] == bz, wide[:, 256 * bz : 256 * bz + 256], part)
                planes.append(part)
        ups.append(dot(take, jnp.concatenate(planes, axis=0).astype(BF16)))
    return jnp.concatenate(ups, axis=0)


def spread_bricks(take, marks, compact, dec_ref):
    for x in range(4):
        spread = dot(take, compact[32 * x : 32 * x + 32], ((0,), (0,)))
        for bx in range(BX):
            one, two = spread[32 * bx : 32 * bx + 16], spread[32 * bx + 16 : 32 * bx + 32]
            for c in range(4):
                block = jnp.where(marks[2 * bx] == c, one, 0.0) + jnp.where(marks[2 * bx + 1] == c, two, 0.0)
                dec_ref[4 * bx + x, :, 256 * c : 256 * c + 256] = block.astype(BF16)


def first_patches(pick, bricks_ref, fe, p1):
    row, col = iota((128, 128), 0), iota((128, 128), 1)
    source = ((row // 2) % 4) * 32 + (row % 2) * 16 + (row // 64) * 8 + (row // 8) % 8
    perm = jnp.where(col == source, 1.0, 0.0).astype(BF16)
    for j in range(4):
        stack = jnp.concatenate([bricks_ref[4 * bx + j] for bx in range(BX)], axis=0)
        moved = dot(perm, stack).reshape(2, 8, 8, 256)
        for plane in range(2):
            fe[2 * j + plane + 1, 1:9, :, 0:256] = moved[plane]
    for px in range(-1, 8):
        for py in range(-1, 8):
            dx, dy = (-1 if px < 0 else 0), (-1 if py < 0 else 0)
            tile = fe[px % 8 + 1, py % 8 + 1, :, 0:256]
            if dx or dy:
                fe[px + 1, py + 1, :, 0:256] = sublane_gather(tile, pick[dx, dy, 0])
            fe[px + 1, py + 1, :, 256:384] = sublane_gather(tile[:, 128:256], pick[dx, dy, -1])
    for tap, (kx, ky) in enumerate(TAPS):
        rows = [fe[2 * x + kx, 2 * y + ky] for x in range(4) for y in range(4)]
        p1[:, tap * 384 : tap * 384 + 384] = jnp.concatenate(rows, axis=0).astype(BF16)


def half_patches(pick, value, ext, patches):
    low = iota((NB, 128), 1) < 64
    for px in range(-1, 5):
        for py in range(-1, 5):
            dx = -1 if px < 0 else (1 if px > 3 else 0)
            dy = -1 if py < 0 else (1 if py > 3 else 0)
            at = ((px % 4) * 4 + py % 4) * 8
            tile = value[at : at + 8]
            if dx or dy:
                ext[px + 1, py + 1, :, 0:256] = sublane_gather(tile, pick[dx, dy, 0])
            else:
                ext[px + 1, py + 1, :, 0:256] = tile
            above = sublane_gather(tile[:, 0:128], pick[dx, dy, 1])
            below = sublane_gather(tile[:, 128:256], pick[dx, dy, -1])
            ext[px + 1, py + 1, :, 256:384] = jnp.where(low, above, below)
    for tap, (kx, ky) in enumerate(TAPS):
        rows = [ext[x + kx, y + ky] for x in range(4) for y in range(4)]
        patches[:, tap * 384 : tap * 384 + 384] = jnp.concatenate(rows, axis=0).astype(BF16)


def halves(parts):
    size = parts[0].shape[0] // 2
    lo, hi = parts[0] + parts[2], parts[1] + parts[3]
    return [(lo[:size], hi[:size]), (lo[size:], hi[size:])]


def fold(pay, lower, upper, target):
    size = lower[0].shape[0]
    is_low = iota((size, 128), 1) < 64
    keep = jnp.where(is_low, lower[0], upper[1])
    turn = jnp.where(is_low, upper[0], lower[1])
    pay[target : target + size, :] = keep + pltpu.roll(turn, 64, 1)


def second_grad(p2, d_second, pay):
    blocks = []
    for tap in range(9):
        full = dot(p2[:, tap * 384 : tap * 384 + 384], d_second, ((0,), (0,)))
        blocks += halves([
            jnp.concatenate([full[320:384, 0:128], full[0:128, 0:128]], axis=0),
            full[0:192, 0:128],
            full[64:256, 128:256],
            full[128:320, 128:256],
        ])
    for at in range(9):
        fold(pay, blocks[at], blocks[at + 9], at * 96)


def first_grad(p1, d_pre, pay):
    blocks = []
    for tap in range(9):
        full = dot(p1[:, tap * 384 : tap * 384 + 384], d_pre, ((0,), (0,)))
        parts = [jnp.concatenate([full[352:384, 0:128], full[0:64, 0:128]], axis=0)]
        for zo in range(1, 4):
            at, lane = 32 * (2 * zo - 1), 128 * (zo // 2)
            parts.append(full[at : at + 96, lane : lane + 128])
        blocks += halves(parts)
    for at in range(9):
        fold(pay, blocks[at], blocks[at + 9], at * 48)


def forward(pick, upstream, bricks_ref, pay2, fe, he, wide1, wide2, p1, p2):
    first_patches(pick, bricks_ref, fe, p1)
    pre = dot(p1[...], wide1[...])
    sig_pre = jax.nn.sigmoid(pre)
    hidden = (pre * sig_pre).astype(BF16)
    half_patches(pick, hidden.astype(F32), he, p2)
    second = dot(p2[...], wide2[...])
    sig = jax.nn.sigmoid(second)
    decoded = (second * sig).astype(BF16)
    d_second = (upstream * (sig * (1.0 + second * (1.0 - sig)))).astype(BF16)
    second_grad(p2, d_second, pay2)
    return sig_pre * (1.0 + pre * (1.0 - sig_pre)), d_second, decoded


def hidden_grad(pick, slope, d_second, de, wide3, p3):
    half_patches(pick, d_second.astype(F32), de, p3)
    d_hidden = dot(p3[...], wide3[...]).astype(BF16)
    return (d_hidden.astype(F32) * slope).astype(BF16)


class Total:
    def __init__(self, rows, factor, pay, out, from_core, mine, from_scene, part, from_z, send, recv):
        self.rows, self.factor = rows, factor
        self.pay, self.out, self.from_core, self.mine = pay, out, from_core, mine
        self.from_scene, self.part, self.from_z, self.send, self.recv = from_scene, part, from_z, send, recv
        tile = lax.axis_index("tile")
        self.scene, self.core, self.z = lax.axis_index("scene"), lax.rem(tile, 2), tile // 2
        self.sibling = {"tile": 2 * self.z + 1 - self.core}

    def chunk(self, half, owner):
        return pl.ds(pl.multiple_of((half * 16 + owner) * self.rows, self.rows), self.rows)

    def copy(self, src, dst, kind, device):
        copy = remote(src, dst, self.send.at[kind], self.recv.at[kind], device)
        copy.start()
        return copy

    def half(self, core):
        size = 16 * self.rows
        return pl.ds(pl.multiple_of(core * size, size), size)

    def owned(self, owner):
        return pl.ds(pl.multiple_of(owner * self.rows, self.rows), self.rows)

    def owner(self, step):
        return lax.rem(self.scene + step, 16)

    def to_core(self):
        self.there = self.copy(self.pay.at[self.half(1 - self.core)], self.from_core, 0, self.sibling)

    def to_scene(self):
        self.there.wait_recv()
        self.mine[...] = (self.pay[self.half(self.core)] + self.from_core[...]).astype(BF16)
        for step in FAR_FIRST:
            owner = self.owner(step)
            self.copy(self.mine.at[self.owned(owner)], self.from_scene.at[self.scene], 1, {"scene": owner})
        self.from_scene[self.scene] = self.mine[self.owned(self.scene)]

    def to_z(self):
        wait_bytes(self.from_scene.at[pl.ds(0, 15)], self.recv.at[1])
        total = self.from_scene[0].astype(F32)
        for k in range(1, 16):
            total = total + self.from_scene[k].astype(F32)
        self.part[...] = total.astype(BF16)
        for step in (4, 3, 5, 2, 6, 1, 7):
            peer = lax.rem(self.z + step, 8)
            self.copy(self.part, self.from_z.at[self.z], 2, {"tile": 2 * peer + self.core})
        self.from_z[self.z] = self.part[...]

    def to_all(self):
        wait_bytes(self.from_z.at[pl.ds(0, 7)], self.recv.at[2])
        total = self.from_z[0].astype(F32)
        for k in range(1, 8):
            total = total + self.from_z[k].astype(F32)
        here = self.out.at[self.chunk(self.core, self.scene)]
        here[...] = (total * self.factor).astype(BF16)
        for step in FAR_FIRST:
            self.copy(here, here, 3, {"scene": self.owner(step)})

    def back(self):
        wait_bytes(self.out.at[pl.ds(0, 15 * self.rows)], self.recv.at[3])
        here = self.out.at[self.half(self.core)]
        self.home = self.copy(here, here, 4, self.sibling)

    def finish(self):
        self.home.wait_recv()
        self.there.wait_send()
        wait_bytes(self.from_scene.at[pl.ds(0, 15)], self.send.at[1])
        wait_bytes(self.from_z.at[pl.ds(0, 7)], self.send.at[2])
        wait_bytes(self.out.at[pl.ds(0, 15 * self.rows)], self.send.at[3])
        self.home.wait_send()


def total_scratch(rows):
    return [
        pltpu.VMEM((32 * rows, 128), F32),
        pltpu.VMEM((16 * rows, 128), F32),
        pltpu.VMEM((16 * rows, 128), BF16),
        pltpu.VMEM((16, rows, 128), BF16),
        pltpu.VMEM((rows, 128), BF16),
        pltpu.VMEM((8, rows, 128), BF16),
        pltpu.SemaphoreType.DMA((5,)),
        pltpu.SemaphoreType.DMA((5,)),
    ]


def train_kernel(factor, assign_hbm, occ_hbm, feats_hbm, w1_hbm, w2_hbm, cot_hbm,
                 out1_ref, out2_ref, dec_ref,
                 assign_ref, owner_ref, occ_ref, feats, w1, w2, cot, packed, stage, bricks,
                 fe, he, de, wide1, wide2, wide3, p1, p2, p3,
                 load_sem, send_sem, recv_sem, *totals):
    tile, scene = lax.axis_index("tile"), lax.axis_index("scene")
    barrier = pltpu.get_barrier_semaphore()
    for step in FAR_FIRST:
        pl.semaphore_signal(barrier, inc=1, device_id={"tile": lax.rem(tile + step, 16)}, device_id_type=MESH)
        pl.semaphore_signal(barrier, inc=1, device_id={"scene": lax.rem(scene + step, 16)}, device_id_type=MESH)
    pieces = [(assign_hbm, assign_ref), (assign_hbm, owner_ref), (occ_hbm, occ_ref)]
    pieces += [(feats_hbm.at[pl.ds(4 * at, 4)], feats.at[pl.ds(4 * at, 4)]) for at in range(4)]
    pieces += [(w1_hbm, w1), (w2_hbm, w2), (cot_hbm, cot)]
    loads = [pltpu.make_async_copy(src, dst, load_sem.at[at]) for at, (src, dst) in enumerate(pieces)]
    for load in loads:
        load.start()
    pay1, pay2 = totals[0], totals[8]
    sum1 = Total(FIRST_ROWS, factor, pay1, out1_ref, *totals[1:8])
    sum2 = Total(SECOND_ROWS, factor, pay2, out2_ref, *totals[9:16])

    for load in loads[:3]:
        load.wait()
    slots = row_codes([occ_ref[tile // 4, by] for by in range(4)])
    for j in range(SCENES):
        if j % 4 == 0:
            loads[3 + j // 4].wait()
        pack_scene(feats, j, slots, packed)
    bricks[tile] = packed[scene_of(assign_ref, tile)]
    for step in FAR_FIRST:
        peer = lax.rem(tile + step, SCENES)
        stage[peer] = packed[scene_of(assign_ref, peer)]
    pl.semaphore_wait(barrier, 30)
    for step in FAR_FIRST:
        peer = lax.rem(tile + step, SCENES)
        remote(stage.at[peer], bricks.at[tile], send_sem, recv_sem, {"tile": peer}).start()

    own = own_codes(occ_ref, owner_ref[...], tile)
    loads[7].wait()
    loads[8].wait()
    banded(w1, w2, wide1, wide2, wide3)
    pick = pickers(own)
    loads[9].wait()
    take, marks = takers(own)
    upstream = upstream_bricks(take, marks, cot)
    pay1[432:512, :] = jnp.zeros((80, 128), F32)
    pay2[864:1024, :] = jnp.zeros((160, 128), F32)
    wait_bytes(bricks.at[pl.ds(0, SCENES - 1)], recv_sem)

    slope, d_second, decoded = forward(pick, upstream, bricks, pay2, fe, he, wide1, wide2, p1, p2)
    sum2.to_core()
    d_pre = hidden_grad(pick, slope, d_second, de, wide3, p3)
    sum2.to_scene()
    first_grad(p1, d_pre, pay1)
    sum1.to_core()
    sum1.to_scene()
    spread_bricks(take, marks, decoded, dec_ref)
    sum2.to_z()
    sum1.to_z()
    sum2.to_all()
    sum1.to_all()
    sum2.back()
    sum1.back()
    sum2.finish()
    sum1.finish()
    wait_bytes(bricks.at[pl.ds(0, SCENES - 1)], send_sem)


def compute_scratch():
    wide = pltpu.VMEM((3456, 256), BF16)
    patch = pltpu.VMEM((128, 3456), BF16)
    return [
        pltpu.VMEM((9, 9, 8, 384), F32),
        pltpu.VMEM((6, 6, 8, 384), F32),
        pltpu.VMEM((6, 6, 8, 384), F32),
        wide, wide, wide, patch, patch, patch,
    ]


def train(assign, occupancy, feats, w1, w2, cot, factor):
    sem = lambda n: pltpu.SemaphoreType.DMA((n,))
    anyspace = pl.BlockSpec(memory_space=pltpu.HBM)
    planes = occupancy.transpose(1, 2, 3, 0)
    return pl.pallas_call(
        functools.partial(train_kernel, factor),
        out_shape=[
            pltpu.VMEM((32 * FIRST_ROWS, 128), BF16),
            pltpu.VMEM((32 * SECOND_ROWS, 128), BF16),
            pltpu.VMEM(cot.shape, BF16),
        ],
        in_specs=[anyspace] * 6,
        out_specs=[vmem()] * 3,
        scratch_shapes=[
            pltpu.SMEM(assign.shape, I32),
            pltpu.VMEM(assign.shape, I32),
            pltpu.VMEM(planes.shape, I32),
            pltpu.VMEM(feats.shape, BF16),
            pltpu.VMEM(w1.shape, BF16),
            pltpu.VMEM(w2.shape, BF16),
            pltpu.VMEM(cot.shape, BF16),
            pltpu.VMEM((SCENES, 32, 256), BF16),
            pltpu.VMEM((SCENES, 32, 256), BF16),
            pltpu.VMEM((SCENES, 32, 256), BF16),
            *compute_scratch(),
            sem(10), pltpu.SemaphoreType.DMA, pltpu.SemaphoreType.DMA,
            *total_scratch(FIRST_ROWS),
            *total_scratch(SECOND_ROWS),
        ],
        compiler_params=pltpu.CompilerParams(collective_id=0, has_side_effects=True, vmem_limit_bytes=VMEM_LIMIT),
        name="train",
    )(*(pltpu.with_memory_space_constraint(x, pltpu.HBM) for x in (assign, planes, feats, w1, w2, cot)))


def unpack_kernel(total1_ref, total2_ref, dec_ref, first_hbm, second_hbm, dec_hbm, first_ref, second_ref, sem):
    stores = [pltpu.make_async_copy(dec_ref, dec_hbm, sem.at[0])]
    stores[0].start()
    row, col = iota((64, 128), 0), iota((64, 128), 1)
    picks = [jnp.where(col == row + 64 * half, 1.0, 0.0).astype(BF16) for half in range(2)]
    jobs = ((second_ref, second_hbm, total2_ref, 864), (first_ref, first_hbm, total1_ref, 432))
    for at, (ref, hbm, total_ref, count) in enumerate(jobs):
        for half in range(2):
            ref[:, count * half : count * half + count] = dot(picks[half], total_ref[0:count], ((1,), (1,)))
        stores.append(pltpu.make_async_copy(ref, hbm, sem.at[1 + at]))
        stores[-1].start()
    for store in stores:
        store.wait()


def unpack(total1, total2, decoded):
    return pl.pallas_call(
        unpack_kernel,
        out_shape=[
            jax.ShapeDtypeStruct((64, 864), F32),
            jax.ShapeDtypeStruct((64, 1728), F32),
            jax.ShapeDtypeStruct(decoded.shape, BF16),
        ],
        in_specs=[vmem(), vmem(), pl.BlockSpec(memory_space=pl.ANY)],
        out_specs=[pl.BlockSpec(memory_space=pl.ANY)] * 3,
        scratch_shapes=[
            pltpu.VMEM((64, 864), F32),
            pltpu.VMEM((64, 1728), F32),
            pltpu.SemaphoreType.DMA((3,)),
        ],
        compiler_params=pltpu.CompilerParams(vmem_limit_bytes=VMEM_LIMIT),
        name="unpack",
    )(total1, total2, decoded)


def per_device(feats, occupancy, assign, w_first, w_second, grad_out):
    factor = 1.0 / math.sqrt(256 * 16 * 16 * 16)
    total1, total2, compact = train(assign, occupancy, feats, w_first.T, w_second.T, grad_out[0], factor)
    grad_first, grad_second, decoded = unpack(total1, total2, compact)
    return decoded[None], grad_first.T, grad_second.T


def solution(mesh):
    return jax.shard_map(
        per_device,
        mesh=mesh,
        in_specs=(
            P("scene", "tile", None, None),
            P("scene", None, None, None),
            P("scene", None),
            P(),
            P(),
            P(("scene", "tile"), None, None, None),
        ),
        out_specs=(P(("scene", "tile"), None, None, None), P(), P()),
        check_vma=False,
    )
```

```python
import functools
import math

import jax
import jax.numpy as jnp
from jax import lax
from jax.experimental import pallas as pl
from jax.experimental.pallas import tpu as pltpu
from jax.sharding import PartitionSpec as P

MESH = pl.DeviceIdType.MESH
F32, BF16, I32 = jnp.float32, jnp.bfloat16, jnp.int32
SCENES, BX, SLOTS, NB = 16, 4, 2, 8
NONE = 16
TAPS = [(kx, ky) for kx in range(3) for ky in range(3)]
SECOND_ROWS, FIRST_ROWS = 32, 16
VMEM_LIMIT = 40 * 1024 * 1024
PLANE = sorted(
    ((dy, dx) for dy in range(4) for dx in range(4) if dy or dx),
    key=lambda d: -(min(d[0], 4 - d[0]) + min(d[1], 4 - d[1])),
)
FAR_FIRST = (8, 7, 9, 6, 10, 5, 11, 4, 12, 3, 13, 2, 14, 1, 15)


def vmem():
    return pl.BlockSpec(memory_space=pltpu.VMEM)


def smem():
    return pl.BlockSpec(memory_space=pltpu.SMEM)


def iota(shape, dim):
    return lax.broadcasted_iota(I32, shape, dim)


def dot(lhs, rhs, dims=((1,), (0,))):
    return lax.dot_general(lhs, rhs, (dims, ((), ())), preferred_element_type=F32)


def remote(src, dst, send, recv, device):
    return pltpu.make_async_remote_copy(
        src_ref=src, dst_ref=dst, send_sem=send, recv_sem=recv, device_id=device, device_id_type=MESH
    )


def plane_peer(scene, place):
    return lax.rem(scene // 4 + place[0], 4) * 4 + lax.rem(lax.rem(scene, 4) + place[1], 4)


def wait_bytes(ref, sem):
    pltpu.make_async_copy(ref, ref, sem).wait()


def row_codes(planes):
    first, last = NONE, -1
    for by in range(4):
        flags = planes[by] > 0
        ids = iota(planes[by].shape, 0) + 4 * by
        first = jnp.minimum(first, jnp.where(flags, ids, NONE))
        last = jnp.maximum(last, jnp.where(flags, ids, -1))
    first = jnp.min(first.astype(F32), axis=0, keepdims=True).astype(I32)
    last = jnp.max(last.astype(F32), axis=0, keepdims=True).astype(I32)
    return first, jnp.where(last > first, last, NONE)


def pack_scene(feats_ref, scene, slots, packed):
    marks = [jnp.broadcast_to(code[:, scene : scene + 1], (8, 256)) for code in slots]
    bys = [mark // 4 for mark in marks]
    bzs = [mark % 4 for mark in marks]
    rows = [[None, None], [None, None]]
    for plane in range(2):
        wide = feats_ref[scene, plane].astype(F32)
        for slot in range(SLOTS):
            acc = jnp.zeros((8, 256), F32)
            for by in range(4):
                line = wide[8 * by : 8 * by + 8]
                part = line[:, 0:256]
                for bz in range(1, 4):
                    part = jnp.where(bzs[slot] == bz, line[:, 256 * bz : 256 * bz + 256], part)
                acc = jnp.where(bys[slot] == by, part, acc)
            rows[slot][plane] = acc
    packed[scene] = jnp.concatenate(rows[0] + rows[1], axis=0).astype(BF16)


def scene_of(assign_ref, target):
    scene = 0
    for j in range(SCENES):
        scene = jnp.where(assign_ref[0, j] == target, j, scene)
    return scene


def own_codes(occ_ref, owner, me):
    codes = []
    for bx in range(BX):
        codes += row_codes([occ_ref[bx, by] for by in range(4)])
    mine = jnp.where(owner == me, jnp.concatenate(codes, axis=0), 0)
    own = jnp.sum(mine.astype(F32), axis=1, keepdims=True).astype(I32)
    return jnp.broadcast_to(own, (NB, 128))


def sublane_gather(value, picker):
    index, hit = picker
    pieces = []
    for at in range(0, value.shape[1], 128):
        got = jnp.take_along_axis(value[:, at : at + 128], index, axis=0)
        pieces.append(jnp.where(hit, got, 0.0))
    return pieces[0] if len(pieces) == 1 else jnp.concatenate(pieces, axis=1)


def pickers(own):
    sub = iota((NB, 128), 0)
    place = jnp.where(own < NONE, (sub // 2) * 64 + (own // 4) * 8 + own % 4, -10000 * (sub + 1))
    each = [jnp.broadcast_to(place[b : b + 1], (NB, 128)) for b in range(NB)]
    pick = {}
    for dx in (-1, 0, 1):
        for dy in (-1, 0, 1):
            for dz in (-1, 0, 1):
                if (dx, dy, dz) == (0, 0, 0):
                    continue
                target = place + (dx * 64 + dy * 8 + dz)
                index = jnp.zeros((NB, 128), I32)
                hit = jnp.zeros((NB, 128), I32)
                for b in range(NB):
                    same = target == each[b]
                    index = jnp.where(same, b, index)
                    hit = jnp.where(same, 1, hit)
                pick[dx, dy, dz] = index, hit > 0
    return pick


def banded(w1_ref, w2_ref, wide1, wide2, wide3):
    wide1[...] = jnp.zeros_like(wide1)
    wide2[...] = jnp.zeros_like(wide2)
    wide3[...] = jnp.zeros_like(wide3)

    def turned(ref):
        return ref[...].astype(F32).T.astype(BF16)

    first, second = turned(w1_ref), turned(w2_ref)
    for tap in range(9):
        base = tap * 384
        w = first[tap * 96 : tap * 96 + 96]
        wide1[base + 352 : base + 384, 0:64] = w[0:32]
        wide1[base : base + 64, 0:64] = w[32:96]
        for zo in range(1, 4):
            at = base + 32 * (2 * zo - 1)
            wide1[at : at + 96, 64 * zo : 64 * zo + 64] = w
        forward = [second[(3 * tap + kz) * 64 : (3 * tap + kz) * 64 + 64] for kz in range(3)]
        backward = [w2_ref[:, (26 - 3 * tap - kz) * 64 : (26 - 3 * tap - kz) * 64 + 64] for kz in range(3)]
        for target, blocks in ((wide2, forward), (wide3, backward)):
            for zo in range(4):
                for kz in range(3):
                    zi = zo + kz - 1
                    at = base + (320 if zi < 0 else 64 * zi)
                    target[at : at + 64, 64 * zo : 64 * zo + 64] = blocks[kz]


def takers(own):
    row, col = iota((32, 128), 0), iota((32, 128), 1)
    start = jnp.where(own < NONE, iota((NB, 128), 0) * 16 + (own // 4) * 4, -10000)
    goal = jnp.concatenate([start] * 4, axis=0) + row // 8
    take = jnp.where(col == goal, 1.0, 0.0).astype(BF16)
    bzs = own % 4
    return take, [jnp.broadcast_to(bzs[b : b + 1, 0:1], (16, 256)) for b in range(NB)]


def upstream_bricks(take, marks, cot_ref):
    ups = []
    for x in range(4):
        planes = []
        for bx in range(BX):
            wide = cot_ref[4 * bx + x].astype(F32)
            for slot in range(SLOTS):
                part = wide[:, 0:256]
                for bz in range(1, 4):
                    part = jnp.where(marks[2 * bx + slot] == bz, wide[:, 256 * bz : 256 * bz + 256], part)
                planes.append(part)
        ups.append(dot(take, jnp.concatenate(planes, axis=0).astype(BF16)))
    return jnp.concatenate(ups, axis=0)


def spread_bricks(take, marks, compact, dec_ref):
    for x in range(4):
        spread = dot(take, compact[32 * x : 32 * x + 32], ((0,), (0,)))
        for bx in range(BX):
            one, two = spread[32 * bx : 32 * bx + 16], spread[32 * bx + 16 : 32 * bx + 32]
            for c in range(4):
                block = jnp.where(marks[2 * bx] == c, one, 0.0) + jnp.where(marks[2 * bx + 1] == c, two, 0.0)
                dec_ref[4 * bx + x, :, 256 * c : 256 * c + 256] = block.astype(BF16)


def first_patches(pick, bricks_ref, fe, p1):
    row, col = iota((128, 128), 0), iota((128, 128), 1)
    source = ((row // 2) % 4) * 32 + (row % 2) * 16 + (row // 64) * 8 + (row // 8) % 8
    perm = jnp.where(col == source, 1.0, 0.0).astype(BF16)
    for j in range(4):
        stack = jnp.concatenate([bricks_ref[4 * bx + j] for bx in range(BX)], axis=0)
        moved = dot(perm, stack).reshape(2, 8, 8, 256)
        for plane in range(2):
            fe[2 * j + plane + 1, 1:9, :, 0:256] = moved[plane]
    for px in range(-1, 8):
        for py in range(-1, 8):
            dx, dy = (-1 if px < 0 else 0), (-1 if py < 0 else 0)
            tile = fe[px % 8 + 1, py % 8 + 1, :, 0:256]
            if dx or dy:
                fe[px + 1, py + 1, :, 0:256] = sublane_gather(tile, pick[dx, dy, 0])
            fe[px + 1, py + 1, :, 256:384] = sublane_gather(tile[:, 128:256], pick[dx, dy, -1])
    for tap, (kx, ky) in enumerate(TAPS):
        rows = [fe[2 * x + kx, 2 * y + ky] for x in range(4) for y in range(4)]
        p1[:, tap * 384 : tap * 384 + 384] = jnp.concatenate(rows, axis=0).astype(BF16)


def half_patches(pick, value, ext, patches):
    low = iota((NB, 128), 1) < 64
    for px in range(-1, 5):
        for py in range(-1, 5):
            dx = -1 if px < 0 else (1 if px > 3 else 0)
            dy = -1 if py < 0 else (1 if py > 3 else 0)
            at = ((px % 4) * 4 + py % 4) * 8
            tile = value[at : at + 8]
            if dx or dy:
                ext[px + 1, py + 1, :, 0:256] = sublane_gather(tile, pick[dx, dy, 0])
            else:
                ext[px + 1, py + 1, :, 0:256] = tile
            above = sublane_gather(tile[:, 0:128], pick[dx, dy, 1])
            below = sublane_gather(tile[:, 128:256], pick[dx, dy, -1])
            ext[px + 1, py + 1, :, 256:384] = jnp.where(low, above, below)
    for tap, (kx, ky) in enumerate(TAPS):
        rows = [ext[x + kx, y + ky] for x in range(4) for y in range(4)]
        patches[:, tap * 384 : tap * 384 + 384] = jnp.concatenate(rows, axis=0).astype(BF16)


def halves(parts):
    size = parts[0].shape[0] // 2
    lo, hi = parts[0] + parts[2], parts[1] + parts[3]
    return [(lo[:size], hi[:size]), (lo[size:], hi[size:])]


def fold(pay, lower, upper, target):
    size = lower[0].shape[0]
    is_low = iota((size, 128), 1) < 64
    keep = jnp.where(is_low, lower[0], upper[1])
    turn = jnp.where(is_low, upper[0], lower[1])
    pay[target : target + size, :] = keep + pltpu.roll(turn, 64, 1)


def second_grad(p2, d_second, pay):
    blocks = []
    for tap in range(9):
        full = dot(p2[:, tap * 384 : tap * 384 + 384], d_second, ((0,), (0,)))
        blocks += halves([
            jnp.concatenate([full[320:384, 0:128], full[0:128, 0:128]], axis=0),
            full[0:192, 0:128],
            full[64:256, 128:256],
            full[128:320, 128:256],
        ])
    for at in range(9):
        fold(pay, blocks[at], blocks[at + 9], at * 96)


def first_grad(p1, d_pre, pay):
    blocks = []
    for tap in range(9):
        full = dot(p1[:, tap * 384 : tap * 384 + 384], d_pre, ((0,), (0,)))
        parts = [jnp.concatenate([full[352:384, 0:128], full[0:64, 0:128]], axis=0)]
        for zo in range(1, 4):
            at, lane = 32 * (2 * zo - 1), 128 * (zo // 2)
            parts.append(full[at : at + 96, lane : lane + 128])
        blocks += halves(parts)
    for at in range(9):
        fold(pay, blocks[at], blocks[at + 9], at * 48)


def forward(pick, upstream, bricks_ref, pay2, fe, he, wide1, wide2, p1, p2):
    first_patches(pick, bricks_ref, fe, p1)
    pre = dot(p1[...], wide1[...])
    sig_pre = jax.nn.sigmoid(pre)
    hidden = (pre * sig_pre).astype(BF16)
    half_patches(pick, hidden.astype(F32), he, p2)
    second = dot(p2[...], wide2[...])
    sig = jax.nn.sigmoid(second)
    decoded = (second * sig).astype(BF16)
    d_second = (upstream * (sig * (1.0 + second * (1.0 - sig)))).astype(BF16)
    second_grad(p2, d_second, pay2)
    return sig_pre * (1.0 + pre * (1.0 - sig_pre)), d_second, decoded


def hidden_grad(pick, slope, d_second, de, wide3, p3):
    half_patches(pick, d_second.astype(F32), de, p3)
    d_hidden = dot(p3[...], wide3[...]).astype(BF16)
    return (d_hidden.astype(F32) * slope).astype(BF16)


class Total:
    def __init__(self, rows, factor, pay, out, from_core, mine, from_scene, part, from_z, send, recv):
        self.rows, self.factor = rows, factor
        self.pay, self.out, self.from_core, self.mine = pay, out, from_core, mine
        self.from_scene, self.part, self.from_z, self.send, self.recv = from_scene, part, from_z, send, recv
        tile = lax.axis_index("tile")
        self.scene, self.core, self.z = lax.axis_index("scene"), lax.rem(tile, 2), tile // 2
        self.sibling = {"tile": 2 * self.z + 1 - self.core}

    def chunk(self, half, owner):
        return pl.ds(pl.multiple_of((half * 16 + owner) * self.rows, self.rows), self.rows)

    def copy(self, src, dst, kind, device):
        copy = remote(src, dst, self.send.at[kind], self.recv.at[kind], device)
        copy.start()
        return copy

    def half(self, core):
        size = 16 * self.rows
        return pl.ds(pl.multiple_of(core * size, size), size)

    def owned(self, owner):
        return pl.ds(pl.multiple_of(owner * self.rows, self.rows), self.rows)

    def to_core(self):
        self.there = self.copy(self.pay.at[self.half(1 - self.core)], self.from_core, 0, self.sibling)

    def to_scene(self):
        self.there.wait_recv()
        self.mine[...] = (self.pay[self.half(self.core)] + self.from_core[...]).astype(BF16)
        for place in PLANE:
            owner = plane_peer(self.scene, place)
            self.copy(self.mine.at[self.owned(owner)], self.from_scene.at[self.scene], 1, {"scene": owner})
        self.from_scene[self.scene] = self.mine[self.owned(self.scene)]

    def to_z(self):
        wait_bytes(self.from_scene.at[pl.ds(0, 15)], self.recv.at[1])
        total = self.from_scene[0].astype(F32)
        for k in range(1, 16):
            total = total + self.from_scene[k].astype(F32)
        self.part[...] = total.astype(BF16)
        for step in (4, 3, 5, 2, 6, 1, 7):
            peer = lax.rem(self.z + step, 8)
            self.copy(self.part, self.from_z.at[self.z], 2, {"tile": 2 * peer + self.core})
        self.from_z[self.z] = self.part[...]

    def to_all(self):
        wait_bytes(self.from_z.at[pl.ds(0, 7)], self.recv.at[2])
        total = self.from_z[0].astype(F32)
        for k in range(1, 8):
            total = total + self.from_z[k].astype(F32)
        here = self.out.at[self.chunk(self.core, self.scene)]
        here[...] = (total * self.factor).astype(BF16)
        for place in PLANE:
            self.copy(here, here, 3, {"scene": plane_peer(self.scene, place)})

    def back(self):
        wait_bytes(self.out.at[pl.ds(0, 15 * self.rows)], self.recv.at[3])
        here = self.out.at[self.half(self.core)]
        self.home = self.copy(here, here, 4, self.sibling)

    def finish(self):
        self.home.wait_recv()
        self.there.wait_send()
        wait_bytes(self.from_scene.at[pl.ds(0, 15)], self.send.at[1])
        wait_bytes(self.from_z.at[pl.ds(0, 7)], self.send.at[2])
        wait_bytes(self.out.at[pl.ds(0, 15 * self.rows)], self.send.at[3])
        self.home.wait_send()


def total_scratch(rows):
    return [
        pltpu.VMEM((32 * rows, 128), F32),
        pltpu.VMEM((16 * rows, 128), F32),
        pltpu.VMEM((16 * rows, 128), BF16),
        pltpu.VMEM((16, rows, 128), BF16),
        pltpu.VMEM((rows, 128), BF16),
        pltpu.VMEM((8, rows, 128), BF16),
        pltpu.SemaphoreType.DMA((5,)),
        pltpu.SemaphoreType.DMA((5,)),
    ]


def train_kernel(factor, assign_hbm, occ_hbm, feats_hbm, w1_hbm, w2_hbm, cot_hbm,
                 out1_ref, out2_ref, dec_ref,
                 assign_ref, owner_ref, occ_ref, feats, w1, w2, cot, packed, stage, bricks,
                 fe, he, de, wide1, wide2, wide3, p1, p2, p3,
                 load_sem, send_sem, recv_sem, *totals):
    tile, scene = lax.axis_index("tile"), lax.axis_index("scene")
    barrier = pltpu.get_barrier_semaphore()
    for step, place in zip(FAR_FIRST, PLANE):
        pl.semaphore_signal(barrier, inc=1, device_id={"tile": lax.rem(tile + step, 16)}, device_id_type=MESH)
        pl.semaphore_signal(barrier, inc=1, device_id={"scene": plane_peer(scene, place)}, device_id_type=MESH)
    pieces = [(assign_hbm, assign_ref), (assign_hbm, owner_ref), (occ_hbm, occ_ref)]
    pieces += [(feats_hbm.at[pl.ds(4 * at, 4)], feats.at[pl.ds(4 * at, 4)]) for at in range(4)]
    pieces += [(w1_hbm, w1), (w2_hbm, w2), (cot_hbm, cot)]
    loads = [pltpu.make_async_copy(src, dst, load_sem.at[at]) for at, (src, dst) in enumerate(pieces)]
    for load in loads:
        load.start()
    pay1, pay2 = totals[0], totals[8]
    sum1 = Total(FIRST_ROWS, factor, pay1, out1_ref, *totals[1:8])
    sum2 = Total(SECOND_ROWS, factor, pay2, out2_ref, *totals[9:16])

    for load in loads[:3]:
        load.wait()
    slots = row_codes([occ_ref[tile // 4, by] for by in range(4)])
    for j in range(SCENES):
        if j % 4 == 0:
            loads[3 + j // 4].wait()
        pack_scene(feats, j, slots, packed)
    bricks[tile] = packed[scene_of(assign_ref, tile)]
    for step in FAR_FIRST:
        peer = lax.rem(tile + step, SCENES)
        stage[peer] = packed[scene_of(assign_ref, peer)]
    pl.semaphore_wait(barrier, 30)
    for step in FAR_FIRST:
        peer = lax.rem(tile + step, SCENES)
        remote(stage.at[peer], bricks.at[tile], send_sem, recv_sem, {"tile": peer}).start()

    own = own_codes(occ_ref, owner_ref[...], tile)
    loads[7].wait()
    loads[8].wait()
    banded(w1, w2, wide1, wide2, wide3)
    pick = pickers(own)
    loads[9].wait()
    take, marks = takers(own)
    upstream = upstream_bricks(take, marks, cot)
    pay1[432:512, :] = jnp.zeros((80, 128), F32)
    pay2[864:1024, :] = jnp.zeros((160, 128), F32)
    wait_bytes(bricks.at[pl.ds(0, SCENES - 1)], recv_sem)

    slope, d_second, decoded = forward(pick, upstream, bricks, pay2, fe, he, wide1, wide2, p1, p2)
    sum2.to_core()
    d_pre = hidden_grad(pick, slope, d_second, de, wide3, p3)
    first_grad(p1, d_pre, pay1)
    sum1.to_core()
    sum2.to_scene()
    sum1.to_scene()
    spread_bricks(take, marks, decoded, dec_ref)
    sum2.to_z()
    sum1.to_z()
    sum2.to_all()
    sum1.to_all()
    sum2.back()
    sum1.back()
    sum2.finish()
    sum1.finish()
    wait_bytes(bricks.at[pl.ds(0, SCENES - 1)], send_sem)


def compute_scratch():
    wide = pltpu.VMEM((3456, 256), BF16)
    patch = pltpu.VMEM((128, 3456), BF16)
    return [
        pltpu.VMEM((9, 9, 8, 384), F32),
        pltpu.VMEM((6, 6, 8, 384), F32),
        pltpu.VMEM((6, 6, 8, 384), F32),
        wide, wide, wide, patch, patch, patch,
    ]


def train(assign, occupancy, feats, w1, w2, cot, factor):
    sem = lambda n: pltpu.SemaphoreType.DMA((n,))
    anyspace = pl.BlockSpec(memory_space=pltpu.HBM)
    planes = occupancy.transpose(1, 2, 3, 0)
    return pl.pallas_call(
        functools.partial(train_kernel, factor),
        out_shape=[
            pltpu.VMEM((32 * FIRST_ROWS, 128), BF16),
            pltpu.VMEM((32 * SECOND_ROWS, 128), BF16),
            pltpu.VMEM(cot.shape, BF16),
        ],
        in_specs=[anyspace] * 6,
        out_specs=[vmem()] * 3,
        scratch_shapes=[
            pltpu.SMEM(assign.shape, I32),
            pltpu.VMEM(assign.shape, I32),
            pltpu.VMEM(planes.shape, I32),
            pltpu.VMEM(feats.shape, BF16),
            pltpu.VMEM(w1.shape, BF16),
            pltpu.VMEM(w2.shape, BF16),
            pltpu.VMEM(cot.shape, BF16),
            pltpu.VMEM((SCENES, 32, 256), BF16),
            pltpu.VMEM((SCENES, 32, 256), BF16),
            pltpu.VMEM((SCENES, 32, 256), BF16),
            *compute_scratch(),
            sem(10), pltpu.SemaphoreType.DMA, pltpu.SemaphoreType.DMA,
            *total_scratch(FIRST_ROWS),
            *total_scratch(SECOND_ROWS),
        ],
        compiler_params=pltpu.CompilerParams(collective_id=0, has_side_effects=True, vmem_limit_bytes=VMEM_LIMIT),
        name="train",
    )(*(pltpu.with_memory_space_constraint(x, pltpu.HBM) for x in (assign, planes, feats, w1, w2, cot)))


def unpack_kernel(total1_ref, total2_ref, dec_ref, first_hbm, second_hbm, dec_hbm, first_ref, second_ref, sem):
    stores = [pltpu.make_async_copy(dec_ref, dec_hbm, sem.at[0])]
    stores[0].start()
    row, col = iota((64, 128), 0), iota((64, 128), 1)
    picks = [jnp.where(col == row + 64 * half, 1.0, 0.0).astype(BF16) for half in range(2)]
    jobs = ((second_ref, second_hbm, total2_ref, 864), (first_ref, first_hbm, total1_ref, 432))
    for at, (ref, hbm, total_ref, count) in enumerate(jobs):
        for half in range(2):
            ref[:, count * half : count * half + count] = dot(picks[half], total_ref[0:count], ((1,), (1,)))
        stores.append(pltpu.make_async_copy(ref, hbm, sem.at[1 + at]))
        stores[-1].start()
    for store in stores:
        store.wait()


def unpack(total1, total2, decoded):
    return pl.pallas_call(
        unpack_kernel,
        out_shape=[
            jax.ShapeDtypeStruct((64, 864), F32),
            jax.ShapeDtypeStruct((64, 1728), F32),
            jax.ShapeDtypeStruct(decoded.shape, BF16),
        ],
        in_specs=[vmem(), vmem(), pl.BlockSpec(memory_space=pl.ANY)],
        out_specs=[pl.BlockSpec(memory_space=pl.ANY)] * 3,
        scratch_shapes=[
            pltpu.VMEM((64, 864), F32),
            pltpu.VMEM((64, 1728), F32),
            pltpu.SemaphoreType.DMA((3,)),
        ],
        compiler_params=pltpu.CompilerParams(vmem_limit_bytes=VMEM_LIMIT),
        name="unpack",
    )(total1, total2, decoded)


def per_device(feats, occupancy, assign, w_first, w_second, grad_out):
    factor = 1.0 / math.sqrt(256 * 16 * 16 * 16)
    total1, total2, compact = train(assign, occupancy, feats, w_first.T, w_second.T, grad_out[0], factor)
    grad_first, grad_second, decoded = unpack(total1, total2, compact)
    return decoded[None], grad_first.T, grad_second.T


def solution(mesh):
    return jax.shard_map(
        per_device,
        mesh=mesh,
        in_specs=(
            P("scene", "tile", None, None),
            P("scene", None, None, None),
            P("scene", None),
            P(),
            P(),
            P(("scene", "tile"), None, None, None),
        ),
        out_specs=(P(("scene", "tile"), None, None, None), P(), P()),
        check_vma=False,
    )
```

```python
import functools
import math

import jax
import jax.numpy as jnp
from jax import lax
from jax.experimental import pallas as pl
from jax.experimental.pallas import tpu as pltpu
from jax.sharding import PartitionSpec as P

MESH = pl.DeviceIdType.MESH
F32, BF16, I32 = jnp.float32, jnp.bfloat16, jnp.int32
SCENES, BX, SLOTS, NB = 16, 4, 2, 8
NONE = 16
TAPS = [(kx, ky) for kx in range(3) for ky in range(3)]
SECOND_ROWS, FIRST_ROWS = 32, 16
VMEM_LIMIT = 40 * 1024 * 1024
PLANE = sorted(
    ((dy, dx) for dy in range(4) for dx in range(4) if dy or dx),
    key=lambda d: -(min(d[0], 4 - d[0]) + min(d[1], 4 - d[1])),
)
FAR_FIRST = (8, 7, 9, 6, 10, 5, 11, 4, 12, 3, 13, 2, 14, 1, 15)


def vmem():
    return pl.BlockSpec(memory_space=pltpu.VMEM)


def smem():
    return pl.BlockSpec(memory_space=pltpu.SMEM)


def iota(shape, dim):
    return lax.broadcasted_iota(I32, shape, dim)


def dot(lhs, rhs, dims=((1,), (0,))):
    return lax.dot_general(lhs, rhs, (dims, ((), ())), preferred_element_type=F32)


def remote(src, dst, send, recv, device):
    return pltpu.make_async_remote_copy(
        src_ref=src, dst_ref=dst, send_sem=send, recv_sem=recv, device_id=device, device_id_type=MESH
    )


def plane_peer(scene, place):
    return lax.rem(scene // 4 + place[0], 4) * 4 + lax.rem(lax.rem(scene, 4) + place[1], 4)


def wait_bytes(ref, sem):
    pltpu.make_async_copy(ref, ref, sem).wait()


def row_codes(planes):
    first, last = NONE, -1
    for by in range(4):
        flags = planes[by] > 0
        ids = iota(planes[by].shape, 0) + 4 * by
        first = jnp.minimum(first, jnp.where(flags, ids, NONE))
        last = jnp.maximum(last, jnp.where(flags, ids, -1))
    first = jnp.min(first.astype(F32), axis=0, keepdims=True).astype(I32)
    last = jnp.max(last.astype(F32), axis=0, keepdims=True).astype(I32)
    return first, jnp.where(last > first, last, NONE)


def pack_scene(feats_ref, scene, slots, packed):
    marks = [jnp.broadcast_to(code[:, scene : scene + 1], (8, 256)) for code in slots]
    bys = [mark // 4 for mark in marks]
    bzs = [mark % 4 for mark in marks]
    rows = [[None, None], [None, None]]
    for plane in range(2):
        wide = feats_ref[scene, plane].astype(F32)
        for slot in range(SLOTS):
            acc = jnp.zeros((8, 256), F32)
            for by in range(4):
                line = wide[8 * by : 8 * by + 8]
                part = line[:, 0:256]
                for bz in range(1, 4):
                    part = jnp.where(bzs[slot] == bz, line[:, 256 * bz : 256 * bz + 256], part)
                acc = jnp.where(bys[slot] == by, part, acc)
            rows[slot][plane] = acc
    packed[scene] = jnp.concatenate(rows[0] + rows[1], axis=0).astype(BF16)


def scene_of(assign_ref, target):
    scene = 0
    for j in range(SCENES):
        scene = jnp.where(assign_ref[0, j] == target, j, scene)
    return scene


def own_codes(occ_ref, owner, me):
    codes = []
    for bx in range(BX):
        codes += row_codes([occ_ref[bx, by] for by in range(4)])
    mine = jnp.where(owner == me, jnp.concatenate(codes, axis=0), 0)
    own = jnp.sum(mine.astype(F32), axis=1, keepdims=True).astype(I32)
    return jnp.broadcast_to(own, (NB, 128))


def sublane_gather(value, picker):
    index, hit = picker
    pieces = []
    for at in range(0, value.shape[1], 128):
        got = jnp.take_along_axis(value[:, at : at + 128], index, axis=0)
        pieces.append(jnp.where(hit, got, 0.0))
    return pieces[0] if len(pieces) == 1 else jnp.concatenate(pieces, axis=1)


def pickers(own):
    sub = iota((NB, 128), 0)
    place = jnp.where(own < NONE, (sub // 2) * 64 + (own // 4) * 8 + own % 4, -10000 * (sub + 1))
    each = [jnp.broadcast_to(place[b : b + 1], (NB, 128)) for b in range(NB)]
    pick = {}
    for dx in (-1, 0, 1):
        for dy in (-1, 0, 1):
            for dz in (-1, 0, 1):
                if (dx, dy, dz) == (0, 0, 0):
                    continue
                target = place + (dx * 64 + dy * 8 + dz)
                index = jnp.zeros((NB, 128), I32)
                hit = jnp.zeros((NB, 128), I32)
                for b in range(NB):
                    same = target == each[b]
                    index = jnp.where(same, b, index)
                    hit = jnp.where(same, 1, hit)
                pick[dx, dy, dz] = index, hit > 0
    return pick


def banded(w1_ref, w2_ref, wide1, wide2, wide3):
    wide1[...] = jnp.zeros_like(wide1)
    wide2[...] = jnp.zeros_like(wide2)
    wide3[...] = jnp.zeros_like(wide3)

    def turned(ref):
        return ref[...].astype(F32).T.astype(BF16)

    first, second = turned(w1_ref), turned(w2_ref)
    for tap in range(9):
        base = tap * 384
        w = first[tap * 96 : tap * 96 + 96]
        wide1[base + 352 : base + 384, 0:64] = w[0:32]
        wide1[base : base + 64, 0:64] = w[32:96]
        for zo in range(1, 4):
            at = base + 32 * (2 * zo - 1)
            wide1[at : at + 96, 64 * zo : 64 * zo + 64] = w
        forward = [second[(3 * tap + kz) * 64 : (3 * tap + kz) * 64 + 64] for kz in range(3)]
        backward = [w2_ref[:, (26 - 3 * tap - kz) * 64 : (26 - 3 * tap - kz) * 64 + 64] for kz in range(3)]
        for target, blocks in ((wide2, forward), (wide3, backward)):
            for zo in range(4):
                for kz in range(3):
                    zi = zo + kz - 1
                    at = base + (320 if zi < 0 else 64 * zi)
                    target[at : at + 64, 64 * zo : 64 * zo + 64] = blocks[kz]


def takers(own):
    row, col = iota((32, 128), 0), iota((32, 128), 1)
    start = jnp.where(own < NONE, iota((NB, 128), 0) * 16 + (own // 4) * 4, -10000)
    goal = jnp.concatenate([start] * 4, axis=0) + row // 8
    take = jnp.where(col == goal, 1.0, 0.0).astype(BF16)
    bzs = own % 4
    return take, [jnp.broadcast_to(bzs[b : b + 1, 0:1], (16, 256)) for b in range(NB)]


def upstream_bricks(take, marks, cot_ref):
    ups = []
    for x in range(4):
        planes = []
        for bx in range(BX):
            wide = cot_ref[4 * bx + x].astype(F32)
            for slot in range(SLOTS):
                part = wide[:, 0:256]
                for bz in range(1, 4):
                    part = jnp.where(marks[2 * bx + slot] == bz, wide[:, 256 * bz : 256 * bz + 256], part)
                planes.append(part)
        ups.append(dot(take, jnp.concatenate(planes, axis=0).astype(BF16)))
    return jnp.concatenate(ups, axis=0)


def spread_bricks(take, marks, compact, dec_ref):
    for x in range(4):
        spread = dot(take, compact[32 * x : 32 * x + 32], ((0,), (0,)))
        for bx in range(BX):
            one, two = spread[32 * bx : 32 * bx + 16], spread[32 * bx + 16 : 32 * bx + 32]
            for c in range(4):
                block = jnp.where(marks[2 * bx] == c, one, 0.0) + jnp.where(marks[2 * bx + 1] == c, two, 0.0)
                dec_ref[4 * bx + x, :, 256 * c : 256 * c + 256] = block.astype(BF16)


def first_patches(pick, bricks_ref, fe, p1):
    row, col = iota((128, 128), 0), iota((128, 128), 1)
    source = ((row // 2) % 4) * 32 + (row % 2) * 16 + (row // 64) * 8 + (row // 8) % 8
    perm = jnp.where(col == source, 1.0, 0.0).astype(BF16)
    for j in range(4):
        stack = jnp.concatenate([bricks_ref[4 * bx + j] for bx in range(BX)], axis=0)
        moved = dot(perm, stack).reshape(2, 8, 8, 256)
        for plane in range(2):
            fe[2 * j + plane + 1, 1:9, :, 0:256] = moved[plane]
    for px in range(-1, 8):
        for py in range(-1, 8):
            dx, dy = (-1 if px < 0 else 0), (-1 if py < 0 else 0)
            tile = fe[px % 8 + 1, py % 8 + 1, :, 0:256]
            if dx or dy:
                fe[px + 1, py + 1, :, 0:256] = sublane_gather(tile, pick[dx, dy, 0])
            fe[px + 1, py + 1, :, 256:384] = sublane_gather(tile[:, 128:256], pick[dx, dy, -1])
    for tap, (kx, ky) in enumerate(TAPS):
        rows = [fe[2 * x + kx, 2 * y + ky] for x in range(4) for y in range(4)]
        p1[:, tap * 384 : tap * 384 + 384] = jnp.concatenate(rows, axis=0).astype(BF16)


def half_patches(pick, value, ext, patches):
    low = iota((NB, 128), 1) < 64
    for px in range(-1, 5):
        for py in range(-1, 5):
            dx = -1 if px < 0 else (1 if px > 3 else 0)
            dy = -1 if py < 0 else (1 if py > 3 else 0)
            at = ((px % 4) * 4 + py % 4) * 8
            tile = value[at : at + 8]
            if dx or dy:
                ext[px + 1, py + 1, :, 0:256] = sublane_gather(tile, pick[dx, dy, 0])
            else:
                ext[px + 1, py + 1, :, 0:256] = tile
            above = sublane_gather(tile[:, 0:128], pick[dx, dy, 1])
            below = sublane_gather(tile[:, 128:256], pick[dx, dy, -1])
            ext[px + 1, py + 1, :, 256:384] = jnp.where(low, above, below)
    for tap, (kx, ky) in enumerate(TAPS):
        rows = [ext[x + kx, y + ky] for x in range(4) for y in range(4)]
        patches[:, tap * 384 : tap * 384 + 384] = jnp.concatenate(rows, axis=0).astype(BF16)


def halves(parts):
    size = parts[0].shape[0] // 2
    lo, hi = parts[0] + parts[2], parts[1] + parts[3]
    return [(lo[:size], hi[:size]), (lo[size:], hi[size:])]


def fold(pay, lower, upper, target):
    size = lower[0].shape[0]
    is_low = iota((size, 128), 1) < 64
    keep = jnp.where(is_low, lower[0], upper[1])
    turn = jnp.where(is_low, upper[0], lower[1])
    pay[target : target + size, :] = keep + pltpu.roll(turn, 64, 1)


def second_grad(p2, d_second, pay):
    blocks = []
    for tap in range(9):
        full = dot(p2[:, tap * 384 : tap * 384 + 384], d_second, ((0,), (0,)))
        blocks += halves([
            jnp.concatenate([full[320:384, 0:128], full[0:128, 0:128]], axis=0),
            full[0:192, 0:128],
            full[64:256, 128:256],
            full[128:320, 128:256],
        ])
    for at in range(9):
        fold(pay, blocks[at], blocks[at + 9], at * 96)


def first_grad(p1, d_pre, pay):
    blocks = []
    for tap in range(9):
        full = dot(p1[:, tap * 384 : tap * 384 + 384], d_pre, ((0,), (0,)))
        parts = [jnp.concatenate([full[352:384, 0:128], full[0:64, 0:128]], axis=0)]
        for zo in range(1, 4):
            at, lane = 32 * (2 * zo - 1), 128 * (zo // 2)
            parts.append(full[at : at + 96, lane : lane + 128])
        blocks += halves(parts)
    for at in range(9):
        fold(pay, blocks[at], blocks[at + 9], at * 48)


def forward(pick, upstream, bricks_ref, pay2, fe, he, wide1, wide2, p1, p2):
    first_patches(pick, bricks_ref, fe, p1)
    pre = dot(p1[...], wide1[...])
    sig_pre = jax.nn.sigmoid(pre)
    hidden = (pre * sig_pre).astype(BF16)
    half_patches(pick, hidden.astype(F32), he, p2)
    second = dot(p2[...], wide2[...])
    sig = jax.nn.sigmoid(second)
    decoded = (second * sig).astype(BF16)
    d_second = (upstream * (sig * (1.0 + second * (1.0 - sig)))).astype(BF16)
    second_grad(p2, d_second, pay2)
    return sig_pre * (1.0 + pre * (1.0 - sig_pre)), d_second, decoded


def hidden_grad(pick, slope, d_second, de, wide3, p3):
    half_patches(pick, d_second.astype(F32), de, p3)
    d_hidden = dot(p3[...], wide3[...]).astype(BF16)
    return (d_hidden.astype(F32) * slope).astype(BF16)


class Total:
    def __init__(self, rows, factor, pay, out, from_core, mine, from_scene, part, from_z, send, recv):
        self.rows, self.factor = rows, factor
        self.pay, self.out, self.from_core, self.mine = pay, out, from_core, mine
        self.from_scene, self.part, self.from_z, self.send, self.recv = from_scene, part, from_z, send, recv
        tile = lax.axis_index("tile")
        self.scene, self.core, self.z = lax.axis_index("scene"), lax.rem(tile, 2), tile // 2
        self.sibling = {"tile": 2 * self.z + 1 - self.core}

    def chunk(self, half, owner):
        return pl.ds(pl.multiple_of((half * 16 + owner) * self.rows, self.rows), self.rows)

    def copy(self, src, dst, kind, device):
        copy = remote(src, dst, self.send.at[kind], self.recv.at[kind], device)
        copy.start()
        return copy

    def half(self, core):
        size = 16 * self.rows
        return pl.ds(pl.multiple_of(core * size, size), size)

    def owned(self, owner):
        return pl.ds(pl.multiple_of(owner * self.rows, self.rows), self.rows)

    def to_core(self):
        self.there = self.copy(self.pay.at[self.half(1 - self.core)], self.from_core, 0, self.sibling)

    def to_scene(self):
        self.there.wait_recv()
        self.mine[...] = (self.pay[self.half(self.core)] + self.from_core[...]).astype(BF16)
        for place in PLANE:
            owner = plane_peer(self.scene, place)
            self.copy(self.mine.at[self.owned(owner)], self.from_scene.at[self.scene], 1, {"scene": owner})
        self.from_scene[self.scene] = self.mine[self.owned(self.scene)]

    def to_z(self):
        wait_bytes(self.from_scene.at[pl.ds(0, 15)], self.recv.at[1])
        total = self.from_scene[0].astype(F32)
        for k in range(1, 16):
            total = total + self.from_scene[k].astype(F32)
        self.part[...] = total.astype(BF16)
        for step in (4, 3, 5, 2, 6, 1, 7):
            peer = lax.rem(self.z + step, 8)
            self.copy(self.part, self.from_z.at[self.z], 2, {"tile": 2 * peer + self.core})
        self.from_z[self.z] = self.part[...]

    def to_all(self):
        wait_bytes(self.from_z.at[pl.ds(0, 7)], self.recv.at[2])
        total = self.from_z[0].astype(F32)
        for k in range(1, 8):
            total = total + self.from_z[k].astype(F32)
        here = self.out.at[self.chunk(self.core, self.scene)]
        here[...] = (total * self.factor).astype(BF16)
        for place in PLANE:
            self.copy(here, here, 3, {"scene": plane_peer(self.scene, place)})

    def back(self):
        wait_bytes(self.out.at[pl.ds(0, 15 * self.rows)], self.recv.at[3])
        here = self.out.at[self.half(self.core)]
        self.home = self.copy(here, here, 4, self.sibling)

    def finish(self):
        self.home.wait_recv()
        self.there.wait_send()
        wait_bytes(self.from_scene.at[pl.ds(0, 15)], self.send.at[1])
        wait_bytes(self.from_z.at[pl.ds(0, 7)], self.send.at[2])
        wait_bytes(self.out.at[pl.ds(0, 15 * self.rows)], self.send.at[3])
        self.home.wait_send()


def turn(total_ref, count, ref):
    row, col = iota((64, 128), 0), iota((64, 128), 1)
    for half in range(2):
        pick = jnp.where(col == row + 64 * half, 1.0, 0.0).astype(BF16)
        ref[:, count * half : count * half + count] = dot(pick, total_ref[0:count], ((1,), (1,)))


def total_scratch(rows):
    return [
        pltpu.VMEM((32 * rows, 128), F32),
        pltpu.VMEM((16 * rows, 128), F32),
        pltpu.VMEM((16 * rows, 128), BF16),
        pltpu.VMEM((16, rows, 128), BF16),
        pltpu.VMEM((rows, 128), BF16),
        pltpu.VMEM((8, rows, 128), BF16),
        pltpu.SemaphoreType.DMA((5,)),
        pltpu.SemaphoreType.DMA((5,)),
    ]


def train_kernel(factor, assign_hbm, occ_hbm, feats_hbm, w1_hbm, w2_hbm, cot_hbm,
                 out1_ref, second_ref, dec_ref,
                 assign_ref, owner_ref, occ_ref, feats, w1, w2, cot, packed, stage, bricks,
                 fe, he, de, wide1, wide2, wide3, p1, p2, p3,
                 out2, load_sem, send_sem, recv_sem, *totals):
    tile, scene = lax.axis_index("tile"), lax.axis_index("scene")
    barrier = pltpu.get_barrier_semaphore()
    for step, place in zip(FAR_FIRST, PLANE):
        pl.semaphore_signal(barrier, inc=1, device_id={"tile": lax.rem(tile + step, 16)}, device_id_type=MESH)
        pl.semaphore_signal(barrier, inc=1, device_id={"scene": plane_peer(scene, place)}, device_id_type=MESH)
    pieces = [(assign_hbm, assign_ref), (assign_hbm, owner_ref), (occ_hbm, occ_ref)]
    pieces += [(feats_hbm.at[pl.ds(4 * at, 4)], feats.at[pl.ds(4 * at, 4)]) for at in range(4)]
    pieces += [(w1_hbm, w1), (w2_hbm, w2), (cot_hbm, cot)]
    loads = [pltpu.make_async_copy(src, dst, load_sem.at[at]) for at, (src, dst) in enumerate(pieces)]
    for load in loads:
        load.start()
    pay1, pay2 = totals[0], totals[8]
    sum1 = Total(FIRST_ROWS, factor, pay1, out1_ref, *totals[1:8])
    sum2 = Total(SECOND_ROWS, factor, pay2, out2, *totals[9:16])

    for load in loads[:3]:
        load.wait()
    slots = row_codes([occ_ref[tile // 4, by] for by in range(4)])
    for j in range(SCENES):
        if j % 4 == 0:
            loads[3 + j // 4].wait()
        pack_scene(feats, j, slots, packed)
    bricks[tile] = packed[scene_of(assign_ref, tile)]
    for step in FAR_FIRST:
        peer = lax.rem(tile + step, SCENES)
        stage[peer] = packed[scene_of(assign_ref, peer)]
    pl.semaphore_wait(barrier, 30)
    for step in FAR_FIRST:
        peer = lax.rem(tile + step, SCENES)
        remote(stage.at[peer], bricks.at[tile], send_sem, recv_sem, {"tile": peer}).start()

    own = own_codes(occ_ref, owner_ref[...], tile)
    loads[7].wait()
    loads[8].wait()
    banded(w1, w2, wide1, wide2, wide3)
    pick = pickers(own)
    loads[9].wait()
    take, marks = takers(own)
    upstream = upstream_bricks(take, marks, cot)
    pay1[432:512, :] = jnp.zeros((80, 128), F32)
    pay2[864:1024, :] = jnp.zeros((160, 128), F32)
    wait_bytes(bricks.at[pl.ds(0, SCENES - 1)], recv_sem)

    slope, d_second, decoded = forward(pick, upstream, bricks, pay2, fe, he, wide1, wide2, p1, p2)
    sum2.to_core()
    d_pre = hidden_grad(pick, slope, d_second, de, wide3, p3)
    first_grad(p1, d_pre, pay1)
    sum1.to_core()
    sum2.to_scene()
    sum1.to_scene()
    spread_bricks(take, marks, decoded, dec_ref)
    sum2.to_z()
    sum1.to_z()
    sum2.to_all()
    sum1.to_all()
    sum2.back()
    sum1.back()
    sum2.finish()
    turn(out2, 864, second_ref)
    sum1.finish()
    wait_bytes(bricks.at[pl.ds(0, SCENES - 1)], send_sem)


def compute_scratch():
    wide = pltpu.VMEM((3456, 256), BF16)
    patch = pltpu.VMEM((128, 3456), BF16)
    return [
        pltpu.VMEM((9, 9, 8, 384), F32),
        pltpu.VMEM((6, 6, 8, 384), F32),
        pltpu.VMEM((6, 6, 8, 384), F32),
        wide, wide, wide, patch, patch, patch,
    ]


def train(assign, occupancy, feats, w1, w2, cot, factor):
    sem = lambda n: pltpu.SemaphoreType.DMA((n,))
    anyspace = pl.BlockSpec(memory_space=pltpu.HBM)
    planes = occupancy.transpose(1, 2, 3, 0)
    return pl.pallas_call(
        functools.partial(train_kernel, factor),
        out_shape=[
            pltpu.VMEM((32 * FIRST_ROWS, 128), BF16),
            pltpu.VMEM((64, 1728), F32),
            pltpu.VMEM(cot.shape, BF16),
        ],
        in_specs=[anyspace] * 6,
        out_specs=[vmem()] * 3,
        scratch_shapes=[
            pltpu.SMEM(assign.shape, I32),
            pltpu.VMEM(assign.shape, I32),
            pltpu.VMEM(planes.shape, I32),
            pltpu.VMEM(feats.shape, BF16),
            pltpu.VMEM(w1.shape, BF16),
            pltpu.VMEM(w2.shape, BF16),
            pltpu.VMEM(cot.shape, BF16),
            pltpu.VMEM((SCENES, 32, 256), BF16),
            pltpu.VMEM((SCENES, 32, 256), BF16),
            pltpu.VMEM((SCENES, 32, 256), BF16),
            *compute_scratch(),
            pltpu.VMEM((32 * SECOND_ROWS, 128), BF16),
            sem(10), pltpu.SemaphoreType.DMA, pltpu.SemaphoreType.DMA,
            *total_scratch(FIRST_ROWS),
            *total_scratch(SECOND_ROWS),
        ],
        compiler_params=pltpu.CompilerParams(collective_id=0, has_side_effects=True, vmem_limit_bytes=VMEM_LIMIT),
        name="train",
    )(*(pltpu.with_memory_space_constraint(x, pltpu.HBM) for x in (assign, planes, feats, w1, w2, cot)))


def unpack_kernel(total1_ref, second_ref, dec_ref, first_hbm, second_hbm, dec_hbm, first_ref, sem):
    stores = [
        pltpu.make_async_copy(dec_ref, dec_hbm, sem.at[0]),
        pltpu.make_async_copy(second_ref, second_hbm, sem.at[1]),
        pltpu.make_async_copy(first_ref, first_hbm, sem.at[2]),
    ]
    stores[0].start()
    stores[1].start()
    turn(total1_ref, 432, first_ref)
    stores[2].start()
    for store in stores:
        store.wait()


def unpack(total1, second, decoded):
    anyspace = pl.BlockSpec(memory_space=pl.ANY)
    return pl.pallas_call(
        unpack_kernel,
        out_shape=[
            jax.ShapeDtypeStruct((64, 864), F32),
            jax.ShapeDtypeStruct(second.shape, F32),
            jax.ShapeDtypeStruct(decoded.shape, BF16),
        ],
        in_specs=[vmem(), anyspace, anyspace],
        out_specs=[anyspace] * 3,
        scratch_shapes=[pltpu.VMEM((64, 864), F32), pltpu.SemaphoreType.DMA((3,))],
        compiler_params=pltpu.CompilerParams(vmem_limit_bytes=VMEM_LIMIT),
        name="unpack",
    )(total1, second, decoded)


def per_device(feats, occupancy, assign, w_first, w_second, grad_out):
    factor = 1.0 / math.sqrt(256 * 16 * 16 * 16)
    total1, second, planes = train(assign, occupancy, feats, w_first.T, w_second.T, grad_out[0], factor)
    grad_first, grad_second, decoded = unpack(total1, second, planes)
    return decoded[None], grad_first.T, grad_second.T


def solution(mesh):
    return jax.shard_map(
        per_device,
        mesh=mesh,
        in_specs=(
            P("scene", "tile", None, None),
            P("scene", None, None, None),
            P("scene", None),
            P(),
            P(),
            P(("scene", "tile"), None, None, None),
        ),
        out_specs=(P(("scene", "tile"), None, None, None), P(), P()),
        check_vma=False,
    )
```
